32 devices in a mesh: dp: 4 (over y, x), ctx: 8 (over z, core).
Axes of the slice: x: 2, y: 2, z: 4, core: 2. Of those that a mesh axis runs over, the one named last changes fastest.
Arguments:
- hidden_in: bfloat16 [8, 2048, 960], P('dp', 'ctx'), may hold values from -6 to 6
- positions: int32 [8, 2048], P('dp', 'ctx'), may hold values from 0 to 2047, as said below
- attn_gain: bfloat16 [960], P('ctx'), may hold values from 0.099609375 to 1.8984375
- w_query: bfloat16 [960, 960], P('dp', 'ctx'), may hold values from -0.1875 to 0.1875
- key_projection_weight: bfloat16 [960, 320], P('dp', 'ctx'), may hold values from -0.1875 to 0.1875
- w_value: bfloat16 [960, 320], P('dp', 'ctx'), may hold values from -0.1875 to 0.1875
- w_out: bfloat16 [960, 960], P('dp', 'ctx'), may hold values from -2 to 2
- ffn_gain: bfloat16 [960], P('ctx'), may hold values from 0.099609375 to 1.8984375
- w_gate: bfloat16 [960, 2560], P('dp', 'ctx'), may hold values from -0.1875 to 0.1875
- w_up: bfloat16 [960, 2560], P('dp', 'ctx'), may hold values from -0.1875 to 0.1875
- w_down: bfloat16 [2560, 960], P('dp', 'ctx'), may hold values from -0.125 to 0.125
- out_grad: bfloat16 [8, 2048, 960], P('dp', 'ctx'), may hold values from -6 to 6
Outputs:
- layer_out: bfloat16 [8, 2048, 960], P('dp', 'ctx')
- input_grad: bfloat16 [8, 2048, 960], P('dp', 'ctx')
- attn_gain_grad: float32 [960], P('ctx')
- w_query_grad: float32 [960, 960], P('dp', 'ctx')
- w_key_grad: float32 [960, 320], P('dp', 'ctx')
- w_value_grad: float32 [960, 320], P('dp', 'ctx')
- w_out_grad: float32 [960, 960], P('dp', 'ctx')
- ffn_gain_grad: float32 [960], P('ctx')
- w_gate_grad: float32 [960, 2560], P('dp', 'ctx')
- w_up_grad: float32 [960, 2560], P('dp', 'ctx')
- w_down_grad: float32 [2560, 960], P('dp', 'ctx')
The draws below stay inside these ranges and needn't reach their ends.
Inputs may be any that keep to these rules, and one draw needn't show every extreme that they name: Every sequence is packed with documents: positions is 0 at a document's first token and rises by one from token to token within it; the first token of every sequence begins a document, and one sequence is a single document.
All inputs are finite; a program needn't handle non-finite values.
Results may differ from the reference program's by a relative error of at most 0.024.
Values may be sent and summed in bfloat16 or wider, within the bound.
No kernel may reach another device: no remote copies, remote signals or barrier semaphores. Data moves between devices by JAX's collectives and lax.ppermute only.
A program may use at most 320 MiB of HBM per device.

```python
import math
import jax
import jax.numpy as jnp
from jax import lax

D = 960
FF = 2560
QUERY_HEADS = 15
KEY_VALUE_HEADS = 5
HEAD_SIZE = 64
SEQ_LEN = 2048
QW = 960
KW = 320
SEQS = 8


def draw_positions(key, part):
    key = jax.random.fold_in(key, 11)
    first_key, second_key = jax.random.split(key)
    column = jnp.arange(SEQ_LEN, dtype=jnp.int32)[None, :]
    row_number = jnp.arange(SEQS, dtype=jnp.int32)[:, None]
    starts = jax.random.randint(first_key, (SEQS, SEQ_LEN), 0, max(SEQ_LEN // 4, 2)) == 0
    single_doc = jax.random.randint(second_key, (), 0, SEQS)
    starts = starts & (row_number != single_doc) | (column == 0)
    begin_at = lax.cummax(jnp.where(starts, column, 0), axis=1)
    return (column - begin_at).astype(jnp.int32)


def strengthened(values, key, source, target, blocks, factor):
    def block_of(position):
        return (jnp.arange(values.shape[position]) // (values.shape[position] // blocks)).reshape((-1,) + (1,) * (values.ndim - 1 - position))

    near = jax.random.permutation(key, blocks)[block_of(target)]
    second = (block_of(target) + blocks // 2) % blocks
    return jnp.where((block_of(source) == near) | (block_of(source) == second), factor * values, values)


def levels(own_key, extent, shards, smallest, largest):
    level = 1.0
    for position, shards_of in shards:
        heights = jax.random.uniform(jax.random.fold_in(jax.random.fold_in(own_key, 6), position), (shards_of,), jnp.float32, smallest / len(shards), largest / len(shards))
        level = level * jnp.repeat(jnp.exp(heights), extent[position] // shards_of).reshape((-1,) + (1,) * (len(extent) - 1 - position))
    return level


def centred(key, extent, width, limit, cuts=(), kind=jnp.bfloat16):
    factor_of = levels(key, extent, cuts, -0.22, 0.18) if cuts else 1.0
    result = jax.random.normal(key, extent, jnp.float32) * width * factor_of
    return jnp.minimum(jnp.maximum(result, -limit), limit).astype(kind)


def bell_draw_with(own_key, shape, width, limit, cuts, heavy, held_as=jnp.bfloat16):
    array = width * jax.random.normal(own_key, shape, jnp.float32)
    if cuts:
        array = array * levels(own_key, shape, cuts, -0.22, 0.18)
    return jnp.clip(strengthened(array, jax.random.fold_in(own_key, 3), *heavy), -limit, limit).astype(held_as)


def setup_inputs(seed: int = 0) -> dict:
    streams_of = jax.random.split(jax.random.key(seed), 13)
    return {
        "hidden_in": centred(streams_of[0], (SEQS, SEQ_LEN, D), 1.0, 6.0, ((0, 4), (1, 8))),
        "positions": draw_positions(jax.random.fold_in(streams_of[12], 71), 0),
        "attn_gain": jnp.clip(1.0 + 0.18 * jax.random.normal(streams_of[2], (D,), jnp.float32), 0.099609375, 1.8984375).astype(jnp.bfloat16),
        "w_query": centred(streams_of[3], (D, QW), D ** -0.5, 0.1875, ((0, 4), (1, 8))),
        "key_projection_weight": centred(streams_of[4], (D, KW), D ** -0.5, 0.1875, ((0, 4), (1, 8))),
        "w_value": centred(streams_of[5], (D, KW), D ** -0.5, 0.1875, ((0, 4), (1, 8))),
        "w_out": centred(streams_of[6], (QW, D), (max(QW // 128, 1)) ** -0.5, 2.0, ((0, 4), (1, 8))),
        "ffn_gain": jnp.clip(1.0 + 0.18 * jax.random.normal(streams_of[7], (D,), jnp.float32), 0.099609375, 1.8984375).astype(jnp.bfloat16),
        "w_gate": centred(streams_of[8], (D, FF), D ** -0.5, 0.1875, ((0, 4), (1, 8))),
        "w_up": centred(streams_of[9], (D, FF), D ** -0.5, 0.1875, ((0, 4), (1, 8))),
        "w_down": centred(streams_of[10], (FF, D), FF ** -0.5, 0.125, ((0, 4), (1, 8))),
        "out_grad": bell_draw_with(streams_of[11], (SEQS, SEQ_LEN, D), 1.0, 6.0, ((0, 4), (1, 8)), (1, 2, 8, 2.0)),
    }


epsilon = 1e-05
theta_base = 100000.0
causal_masked_score = -1e+30

@jax.custom_vjp
def low(v):
    return lax.optimization_barrier(v.astype(jnp.bfloat16)).astype(jnp.float32)

@jax.custom_vjp
def low_back(v):
    return v

def low_keep(v):
    return (low(v), None)

def low_pass(kept, grad):
    return (grad,)

def back_keep(v):
    return (v, None)

def back_low(kept, grad):
    return (low(grad),)
low.defvjp(low_keep, low_pass)
low_back.defvjp(back_keep, back_low)

def product_full_precision(left_rows, right_rows):
    return jnp.dot(left_rows, right_rows, precision=lax.Precision.HIGHEST)

def rms_norm(value_matrix, gain_row):
    norm_scale = lax.rsqrt(lax.optimization_barrier(jnp.mean(value_matrix * value_matrix, axis=-1, keepdims=True)) + epsilon)
    return value_matrix * norm_scale * gain_row

def rotary_pair_rotation(value_matrix, sequence_positions, heads):
    token_length = value_matrix.shape[0]
    half_size = HEAD_SIZE // 2
    frequency = jnp.power(theta_base, -jnp.arange(half_size, dtype=jnp.float32) * 2.0 / HEAD_SIZE)
    angle_table = sequence_positions.astype(jnp.float32)[:, None] * frequency[None, :]
    cosine_table = jnp.cos(angle_table)[:, None, :]
    sine_table = jnp.sin(angle_table)[:, None, :]
    split_heads = value_matrix.reshape(token_length, heads, HEAD_SIZE)
    first_half = split_heads[..., :half_size]
    second_half = split_heads[..., half_size:]
    turned = jnp.concatenate([first_half * cosine_table - second_half * sine_table, second_half * cosine_table + first_half * sine_table], axis=-1)
    return turned.reshape(token_length, heads * HEAD_SIZE)

def attention(query_matrix, gathered_keys, gathered_values, sequence_positions):
    token_length = query_matrix.shape[0]
    heads_per_group = QUERY_HEADS // KEY_VALUE_HEADS
    block_rows = min(512, token_length)
    query_head_rows = query_matrix.reshape(token_length, KEY_VALUE_HEADS, heads_per_group, HEAD_SIZE)
    key_head_rows = gathered_keys.reshape(token_length, KEY_VALUE_HEADS, HEAD_SIZE)
    value_head_rows = gathered_values.reshape(token_length, KEY_VALUE_HEADS, HEAD_SIZE)
    key_index = jnp.arange(token_length, dtype=jnp.int32)
    score_scale = 1.0 / math.sqrt(HEAD_SIZE)

    def one_block(first_row):
        q_block = lax.dynamic_slice_in_dim(query_head_rows, first_row, block_rows, 0)
        query_index = first_row + jnp.arange(block_rows, dtype=jnp.int32)
        query_pos = lax.dynamic_slice_in_dim(sequence_positions, first_row, block_rows, 0)
        raw_scores = jnp.einsum('qhgd,khd->hgqk', q_block, key_head_rows, precision=lax.Precision.HIGHEST)
        scores = low_back(raw_scores) * score_scale
        allowed = (key_index[None, :] <= query_index[:, None]) & (query_index[:, None] - key_index[None, :] == query_pos[:, None] - sequence_positions[None, :])
        scores = jnp.where(allowed, scores, causal_masked_score)
        row_top = lax.optimization_barrier(jnp.max(scores, axis=-1, keepdims=True))
        expo = jnp.exp(scores - row_top)
        probabilities = expo / lax.optimization_barrier(jnp.sum(expo, axis=-1, keepdims=True))
        block_out = jnp.einsum('hgqk,khd->qhgd', low(probabilities), value_head_rows, precision=lax.Precision.HIGHEST)
        return block_out.reshape(block_rows, QUERY_HEADS * HEAD_SIZE)
    starts = jnp.arange(token_length // block_rows, dtype=jnp.int32) * block_rows
    return lax.map(jax.checkpoint(one_block), starts).reshape(token_length, QUERY_HEADS * HEAD_SIZE)

def layer_sequence(inputs_seq, sequence_positions, attn_gain, w_query, key_projection_weight, w_value, w_out, ffn_gain, w_gate, w_up, w_down):
    first_normed_input = low(rms_norm(inputs_seq, attn_gain))
    query_matrix = low(rotary_pair_rotation(low_back(product_full_precision(first_normed_input, w_query)), sequence_positions, QUERY_HEADS))
    gathered_keys = low(rotary_pair_rotation(low_back(product_full_precision(first_normed_input, key_projection_weight)), sequence_positions, KEY_VALUE_HEADS))
    gathered_values = low(low_back(product_full_precision(first_normed_input, w_value)))
    attended = low(low_back(attention(query_matrix, gathered_keys, gathered_values, sequence_positions)))
    residual_mid = inputs_seq + low_back(product_full_precision(attended, w_out))
    normed_two = low(rms_norm(residual_mid, ffn_gain))
    gate_proj = low_back(product_full_precision(normed_two, w_gate))
    up_proj = low_back(product_full_precision(normed_two, w_up))
    hidden = low(jax.nn.silu(gate_proj) * up_proj)
    return residual_mid + low_back(product_full_precision(hidden, w_down))

def reference(hidden_in, positions, attn_gain, w_query, key_projection_weight, w_value, w_out, ffn_gain, w_gate, w_up, w_down, out_grad):
    inputs_all = hidden_in.astype(jnp.float32)

    def forward(inputs_all, gain_attn, weight_query, weight_key, weight_value, weight_out, gain_ffn, weight_gate, weight_up, weight_down):

        def per_sequence(item_pair):
            inputs_seq, sequence_positions = item_pair
            return layer_sequence(inputs_seq, sequence_positions, gain_attn, weight_query, weight_key, weight_value, weight_out, gain_ffn, weight_gate, weight_up, weight_down)
        return lax.map(jax.checkpoint(per_sequence), (inputs_all, positions))
    outputs, pull_back = jax.vjp(forward, inputs_all, attn_gain.astype(jnp.float32), w_query.astype(jnp.float32), key_projection_weight.astype(jnp.float32), w_value.astype(jnp.float32), w_out.astype(jnp.float32), ffn_gain.astype(jnp.float32), w_gate.astype(jnp.float32), w_up.astype(jnp.float32), w_down.astype(jnp.float32))
    grads = pull_back(out_grad.astype(jnp.float32))
    return (outputs.astype(jnp.bfloat16), grads[0].astype(jnp.bfloat16), grads[1], grads[2], grads[3], grads[4], grads[5], grads[6], grads[7], grads[8], grads[9])
```

```python
import functools

import jax
import jax.numpy as jnp
import numpy as np
from jax import lax
from jax.experimental import pallas as pl
from jax.experimental.pallas import tpu as pltpu
from jax.sharding import PartitionSpec as P

QUERY_HEADS = 15
KEY_VALUE_HEADS = 5
HEAD_SIZE = 64
GROUP = QUERY_HEADS // KEY_VALUE_HEADS
HALF = HEAD_SIZE // 2

epsilon = 1e-05
theta_base = 100000.0
masked_score = -1e30
lowest_top = -1e29
score_scale = 0.125
VMEM_BYTES = 56 * 1024 * 1024

BF = jnp.bfloat16
F32 = jnp.float32


def dot_nn(a, b):
    return lax.dot_general(a, b, (((1,), (0,)), ((), ())), preferred_element_type=F32)


def dot_nt(a, b):
    return lax.dot_general(a, b, (((1,), (1,)), ((), ())), preferred_element_type=F32)


def dot_tn(a, b):
    return lax.dot_general(a, b, (((0,), (0,)), ((), ())), preferred_element_type=F32)


def vmem_spec():
    return pl.BlockSpec(memory_space=pltpu.VMEM)


def smem_spec():
    return pl.BlockSpec(memory_space=pltpu.SMEM)


def params():
    return pltpu.CompilerParams(vmem_limit_bytes=VMEM_BYTES)


def cost(flops, bytes_accessed, transcendentals=0):
    return pl.CostEstimate(
        flops=int(flops), bytes_accessed=int(bytes_accessed), transcendentals=int(transcendentals)
    )


def rotate(value, cosine, sine, limit=None):
    width = value.shape[1]
    lane = lax.broadcasted_iota(jnp.int32, value.shape, 1)
    ahead = pltpu.roll(value, width - HALF, 1)
    behind = pltpu.roll(value, HALF, 1)
    swapped = jnp.where(lane % HEAD_SIZE < HALF, ahead, behind)
    copies = width // 128
    cos_wide = jnp.concatenate([cosine] * copies, axis=1)
    sin_wide = jnp.concatenate([sine] * copies, axis=1)
    turned = value * cos_wide + swapped * sin_wide
    if limit is not None:
        turned = jnp.where(lane < limit, turned, value)
    return turned


def projection_kernel(count, columns, turn, index_ref, x_ref, *rest):
    weights = rest[:count]
    rest = rest[count:]
    if turn:
        cos_ref, sin_ref, out_ref = rest
    else:
        (out_ref,) = rest
    for start in range(0, columns, 256):
        size = min(256, columns - start)
        total = None
        for m in range(count):
            term = dot_nt(x_ref[index_ref[m]], weights[m][start : start + size, :])
            total = term if total is None else total + term
        if turn > start:
            total = rotate(total, cos_ref[...], sin_ref[...], turn - start if turn < start + size else None)
        out_ref[:, start : start + size] = total.astype(out_ref.dtype)


def project(x_blocks, index, weights, out_dtype, tables=None, turn=0):
    count = len(weights)
    rows = x_blocks.shape[1]
    columns = weights[0].shape[0]
    depth = x_blocks.shape[2]
    operands = [index, x_blocks, *weights] + (list(tables) if tables else [])
    return pl.pallas_call(
        functools.partial(projection_kernel, count, columns, turn),
        out_shape=jax.ShapeDtypeStruct((rows, columns), out_dtype),
        in_specs=[smem_spec()] + [vmem_spec()] * (len(operands) - 1),
        out_specs=vmem_spec(),
        compiler_params=params(),
        cost_estimate=cost(2 * rows * columns * depth * count, 2 * columns * depth * count + 4 * rows * columns),
    )(*operands)


def projection_back_kernel(count, columns, index_ref, dy_ref, x_ref, *rest):
    weights = rest[:count]
    dx_ref, dw_ref = rest[count:]
    for m in range(count):
        place = index_ref[m]
        dx_ref[place] = dot_nn(dy_ref[...], weights[m][...])
        for start in range(0, columns, 256):
            size = min(256, columns - start)
            dw_ref[m, start : start + size, :] = dot_tn(
                dy_ref[:, start : start + size], x_ref[place]
            ).astype(BF)


def project_back(dy, x_blocks, index, weights):
    count = len(weights)
    rows, depth = x_blocks.shape[1:]
    columns = weights[0].shape[0]
    return pl.pallas_call(
        functools.partial(projection_back_kernel, count, columns),
        out_shape=(
            jax.ShapeDtypeStruct((count, rows, depth), F32),
            jax.ShapeDtypeStruct((count, columns, depth), BF),
        ),
        in_specs=[smem_spec()] + [vmem_spec()] * (2 + count),
        out_specs=(vmem_spec(), vmem_spec()),
        compiler_params=params(),
        cost_estimate=cost(4 * rows * columns * depth * count, 4 * columns * depth * count + 4 * rows * columns),
    )(index, dy, x_blocks, *weights)


def ffn_kernel(nd, nz, dp_ref, z_ref, n2_ref, dy_ref, *rest):
    gu = rest[:nd]
    down = rest[nd : nd + nz]
    out_ref, dn_ref, dgu_ref, dd_ref = rest[nd + nz :]

    @pl.when(pl.program_id(0) == 0)
    def _():
        out_ref[...] = jnp.zeros_like(out_ref)
        dn_ref[...] = jnp.zeros_like(dn_ref)

    gate = up = grad_hidden = None
    for m in range(nd):
        rows = n2_ref[dp_ref[m]]
        term_g = dot_nt(rows, gu[m][0])
        term_u = dot_nt(rows, gu[m][1])
        gate = term_g if gate is None else gate + term_g
        up = term_u if up is None else up + term_u
    for s in range(nz):
        term = dot_nt(dy_ref[z_ref[s]], down[s][...])
        grad_hidden = term if grad_hidden is None else grad_hidden + term
    sig = jax.nn.sigmoid(gate)
    act = gate * sig
    hidden = (act * up).astype(BF)
    d_gate = (grad_hidden * up * sig * (1.0 + gate * (1.0 - sig))).astype(BF)
    d_up = (grad_hidden * act).astype(BF)
    for s in range(nz):
        place = z_ref[s]
        out_ref[place] += dot_nn(hidden, down[s][...])
        dd_ref[s] = dot_tn(hidden, dy_ref[place]).astype(BF)
    for m in range(nd):
        place = dp_ref[m]
        rows = n2_ref[place]
        dn_ref[place] += dot_nn(d_gate, gu[m][0]) + dot_nn(d_up, gu[m][1])
        dgu_ref[m, 0] = dot_tn(d_gate, rows).astype(BF)
        dgu_ref[m, 1] = dot_tn(d_up, rows).astype(BF)


def feed_forward(n2_blocks, dy_blocks, dp_index, z_index, gu, down):
    nd, nz = len(gu), len(down)
    rows = n2_blocks.shape[1]
    units = gu[0].shape[1]
    chunk = 256
    dl, zl = n2_blocks.shape[2], dy_blocks.shape[2]
    flops = 2 * rows * units * (nd * dl) * 9
    return pl.pallas_call(
        functools.partial(ffn_kernel, nd, nz),
        grid=(units // chunk,),
        out_shape=(
            jax.ShapeDtypeStruct((nz, rows, zl), F32),
            jax.ShapeDtypeStruct((nd, rows, dl), F32),
            jax.ShapeDtypeStruct((nd, 2, units, dl), BF),
            jax.ShapeDtypeStruct((nz, units, zl), BF),
        ),
        in_specs=[smem_spec(), smem_spec()]
        + [
            pl.BlockSpec(n2_blocks.shape, lambda i: (0, 0, 0)),
            pl.BlockSpec(dy_blocks.shape, lambda i: (0, 0, 0)),
        ]
        + [pl.BlockSpec((2, chunk, dl), lambda i: (0, i, 0))] * nd
        + [pl.BlockSpec((chunk, zl), lambda i: (i, 0))] * nz,
        out_specs=(
            pl.BlockSpec((nz, rows, zl), lambda i: (0, 0, 0)),
            pl.BlockSpec((nd, rows, dl), lambda i: (0, 0, 0)),
            pl.BlockSpec((nd, 2, chunk, dl), lambda i: (0, 0, i, 0)),
            pl.BlockSpec((nz, chunk, zl), lambda i: (0, i, 0)),
        ),
        compiler_params=params(),
        cost_estimate=cost(flops, 12 * units * nd * dl, rows * units),
    )(dp_index, z_index, n2_blocks, dy_blocks, *gu, *down)


def group_rows(ref, g):
    return jnp.concatenate(
        [ref[:, (g * GROUP + i) * HEAD_SIZE : (g * GROUP + i + 1) * HEAD_SIZE] for i in range(GROUP)],
        axis=0,
    )


def bias_of(start_ref, first_query, first_key, span, size):
    key = first_key + lax.broadcasted_iota(jnp.int32, (span, size), 1)
    query = first_query + lax.broadcasted_iota(jnp.int32, (span, size), 0)
    allowed = (key <= query) & (key >= start_ref[...])
    return jnp.where(allowed, 0.0, masked_score)


def attend_kernel(span, size, info_ref, start_ref, q_ref, kv_ref, att_ref, lse_ref, acc, top, total):
    first_query = info_ref[0]
    top[...] = jnp.full_like(top, lowest_top)
    total[...] = jnp.zeros_like(total)
    acc[...] = jnp.zeros_like(acc)
    value_at = KEY_VALUE_HEADS * HEAD_SIZE

    def one_block(block, carry):
        first_key = pl.multiple_of(block * size, size)
        bias = bias_of(start_ref, first_query, first_key, span, size)
        bias = jnp.concatenate([bias] * GROUP, axis=0)
        for g in range(KEY_VALUE_HEADS):
            rows = group_rows(q_ref, g) * BF(score_scale)
            keys = kv_ref[pl.ds(first_key, size), g * HEAD_SIZE : (g + 1) * HEAD_SIZE]
            values = kv_ref[
                pl.ds(first_key, size), value_at + g * HEAD_SIZE : value_at + (g + 1) * HEAD_SIZE
            ]
            scores = dot_nt(rows, keys) + bias
            old_top = top[g]
            new_top = jnp.maximum(old_top, jnp.max(scores, axis=1, keepdims=True))
            rescale = jnp.exp(old_top - new_top)
            expo = jnp.exp(scores - new_top)
            total[g] = total[g] * rescale + jnp.sum(expo, axis=1, keepdims=True)
            acc[g] = acc[g] * rescale + dot_nn(expo.astype(BF), values)
            top[g] = new_top
        return carry

    lax.fori_loop(info_ref[1], info_ref[2], one_block, 0)
    lane = lax.broadcasted_iota(jnp.int32, lse_ref.shape, 1)
    lse = jnp.zeros(lse_ref.shape, F32)
    for g in range(KEY_VALUE_HEADS):
        whole = total[g]
        result = (acc[g] * (1.0 / whole)).astype(BF)
        log_total = top[g] + jnp.log(whole)
        for i in range(GROUP):
            h = g * GROUP + i
            att_ref[:, h * HEAD_SIZE : (h + 1) * HEAD_SIZE] = result[i * span : (i + 1) * span]
            lse = jnp.where(lane == h, log_total[i * span : (i + 1) * span], lse)
    lse_ref[...] = lse


def attend(info, start, q, kv, size):
    span = q.shape[0]
    rows = GROUP * span
    length = kv.shape[0]
    return pl.pallas_call(
        functools.partial(attend_kernel, span, size),
        out_shape=(
            jax.ShapeDtypeStruct((span, QUERY_HEADS * HEAD_SIZE), BF),
            jax.ShapeDtypeStruct((span, 128), F32),
        ),
        in_specs=[smem_spec()] + [vmem_spec()] * 3,
        out_specs=(vmem_spec(), vmem_spec()),
        scratch_shapes=[
            pltpu.VMEM((KEY_VALUE_HEADS, rows, HEAD_SIZE), F32),
            pltpu.VMEM((KEY_VALUE_HEADS, rows, 1), F32),
            pltpu.VMEM((KEY_VALUE_HEADS, rows, 1), F32),
        ],
        compiler_params=params(),
        cost_estimate=cost(
            16 * QUERY_HEADS * HEAD_SIZE * span * length,
            4 * length * KEY_VALUE_HEADS * HEAD_SIZE,
            QUERY_HEADS * span * length,
        ),
    )(info, start, q, kv)


def attend_back_kernel(
    span, size, info_ref, start_ref, q_ref, kv_ref, att_ref, datt_ref, lse_ref, cos_ref, sin_ref,
    dq_ref, dkv_ref, dq_acc, q_rows, d_rows, lse_rows, dot_rows,
):
    first_query = info_ref[0]
    value_at = KEY_VALUE_HEADS * HEAD_SIZE
    dq_acc[...] = jnp.zeros_like(dq_acc)
    dkv_ref[...] = jnp.zeros_like(dkv_ref)
    for g in range(KEY_VALUE_HEADS):
        grads = group_rows(datt_ref, g)
        q_rows[g] = group_rows(q_ref, g) * BF(score_scale)
        d_rows[g] = grads
        dot_rows[g] = jnp.sum(
            grads.astype(F32) * group_rows(att_ref, g).astype(F32), axis=1, keepdims=True
        )
        lse_rows[g] = jnp.concatenate(
            [lse_ref[:, g * GROUP + i : g * GROUP + i + 1] for i in range(GROUP)], axis=0
        )

    def one_block(block, carry):
        first_key = pl.multiple_of(block * size, size)
        bias = bias_of(start_ref, first_query, first_key, span, size)
        bias = jnp.concatenate([bias] * GROUP, axis=0)
        for g in range(KEY_VALUE_HEADS):
            k_at, v_at = g * HEAD_SIZE, value_at + g * HEAD_SIZE
            rows = q_rows[g]
            grads = d_rows[g]
            keys = kv_ref[pl.ds(first_key, size), k_at : k_at + HEAD_SIZE]
            values = kv_ref[pl.ds(first_key, size), v_at : v_at + HEAD_SIZE]
            probs = jnp.exp((dot_nt(rows, keys) + bias) - lse_rows[g])
            d_probs = dot_nt(grads, values)
            d_scores = (probs * (d_probs - dot_rows[g])).astype(BF)
            dkv_ref[pl.ds(first_key, size), v_at : v_at + HEAD_SIZE] = dot_tn(
                probs.astype(BF), grads
            ).astype(BF)
            dkv_ref[pl.ds(first_key, size), k_at : k_at + HEAD_SIZE] = dot_tn(d_scores, rows).astype(BF)
            dq_acc[g] += dot_nn(d_scores, keys)
        return carry

    lax.fori_loop(info_ref[1], info_ref[2], one_block, 0)
    cosine, sine = cos_ref[...], -sin_ref[...]
    for start in range(0, QUERY_HEADS + 1, 2):
        parts = []
        for h in (start, start + 1):
            if h < QUERY_HEADS:
                g, i = h // GROUP, h % GROUP
                parts.append(dq_acc[g, i * span : (i + 1) * span] * score_scale)
            else:
                parts.append(jnp.zeros((span, HEAD_SIZE), F32))
        pair = jnp.concatenate(parts, axis=1)
        dq_ref[:, start * HEAD_SIZE : (start + 2) * HEAD_SIZE] = rotate(pair, cosine, sine).astype(BF)


def attend_back(info, start, q, kv, att, datt, lse, cosine, sine, size):
    span = q.shape[0]
    rows = GROUP * span
    length = kv.shape[0]
    per_head = (KEY_VALUE_HEADS, rows, HEAD_SIZE)
    per_row = (KEY_VALUE_HEADS, rows, 1)
    return pl.pallas_call(
        functools.partial(attend_back_kernel, span, size),
        out_shape=(
            jax.ShapeDtypeStruct((span, q.shape[1]), BF),
            jax.ShapeDtypeStruct(kv.shape, BF),
        ),
        in_specs=[smem_spec()] + [vmem_spec()] * 8,
        out_specs=(vmem_spec(), vmem_spec()),
        scratch_shapes=[
            pltpu.VMEM(per_head, F32),
            pltpu.VMEM(per_head, BF),
            pltpu.VMEM(per_head, BF),
            pltpu.VMEM(per_row, F32),
            pltpu.VMEM(per_row, F32),
        ],
        compiler_params=params(),
        cost_estimate=cost(
            40 * QUERY_HEADS * HEAD_SIZE * span * length,
            8 * length * KEY_VALUE_HEADS * HEAD_SIZE,
            QUERY_HEADS * span * length,
        ),
    )(info, start, q, kv, att, datt, lse, cosine, sine)


def norm_scale(value):
    return lax.rsqrt(jnp.mean(value * value, axis=-1, keepdims=True) + epsilon)


def to_blocks(value, count):
    rows, width = value.shape
    return value.reshape(rows, count, width // count).transpose(1, 0, 2)


def from_blocks(value):
    count, rows, width = value.shape
    return value.transpose(1, 0, 2).reshape(rows, count * width)


def on_device(
    hidden_in,
    positions,
    attn_gain,
    w_query,
    key_projection_weight,
    w_value,
    w_out,
    ffn_gain,
    w_gate,
    w_up,
    w_down,
    out_grad,
):
    nd, nc = lax.axis_size("dp"), lax.axis_size("ctx")
    nz = nc // 2
    seqs, span, width = hidden_in.shape
    rows = seqs * span
    length = span * nc
    d, rank = lax.axis_index("dp"), lax.axis_index("ctx")
    z, c = rank // 2, rank % 2
    first = c == 0
    block_size = min(512, length)

    def send(value, to):
        pairs = []
        for di in range(nd):
            for zi in range(nz):
                for ci in range(2):
                    target = to(di, zi, ci)
                    if target is not None:
                        dt, zt, ct = target
                        pairs.append((di * nc + zi * 2 + ci, dt * nc + zt * 2 + ct))
        return lax.ppermute(value, ("dp", "ctx"), pairs)

    def z_shift(value, s):
        return send(value, lambda di, zi, ci: (di, (zi + s) % nz, ci))

    def z_up(value):
        return send(value, lambda di, zi, ci: (di, zi + 1, ci) if zi + 1 < nz else None)

    def z_down(value, s):
        return send(value, lambda di, zi, ci: (di, zi - s, ci) if zi >= s else None)

    def dp_xor(value, m):
        return send(value, lambda di, zi, ci: (di ^ m, zi, ci))

    def core_swap(value):
        return send(value, lambda di, zi, ci: (di, zi, 1 - ci))

    def put(buffer, piece, axis, place):
        return lax.dynamic_update_slice_in_dim(buffer, piece, place, axis)

    def take(value, axis, place):
        return lax.dynamic_index_in_dim(value, place, axis, keepdims=False)

    def gather_z(value, axis):
        shape = list(value.shape)
        shape[axis] = nz
        buffer = put(jnp.zeros(shape, value.dtype), value, axis, z)
        for s in range(1, nz):
            buffer = put(buffer, z_shift(value, s), axis, (z - s) % nz)
        return buffer

    def in_core_order(own, other, axis):
        return jnp.stack([jnp.where(first, own, other), jnp.where(first, other, own)], axis=axis)

    dp_index = jnp.bitwise_xor(d, jnp.arange(nd, dtype=jnp.int32))
    z_index = (z - jnp.arange(nz, dtype=jnp.int32)) % nz

    gains = jnp.stack([attn_gain, ffn_gain]).reshape(2, 1, -1)
    gains = gather_z(gains, 1)
    gains = in_core_order(gains, core_swap(gains), 2).reshape(2, width).astype(F32)
    gain_attn, gain_ffn = gains[0], gains[1]

    def gather_pair(left, right):
        value = jnp.stack([left.T, right.T])[:, None]
        own = gather_z(value, 1)
        own = [own] + [dp_xor(own, m) for m in range(1, nd)]
        whole = []
        for piece in own:
            both = in_core_order(piece, core_swap(piece), 2)
            whole.append(both.reshape(2, -1, piece.shape[-1]))
        return whole

    kv_weights = [w.reshape(-1, w.shape[-1]) for w in gather_pair(key_projection_weight, w_value)]
    qo_weights = gather_pair(w_query, w_out)
    padding = -(QUERY_HEADS * HEAD_SIZE) % 128
    q_weights = [jnp.pad(w[0], ((0, padding), (0, 0))) for w in qo_weights]
    o_weights = [w[1] for w in qo_weights]

    gu_local = jnp.stack([w_gate.T, w_up.T])[:, None]
    gu_own = gather_z(gu_local, 1)
    gu_own = gu_own.reshape(2, -1, gu_own.shape[-1])
    gu_own = [gu_own] + [dp_xor(gu_own, m) for m in range(1, nd)]
    gu_other = [core_swap(piece) for piece in gu_own]

    units = w_gate.shape[1]
    down_cut = w_down.reshape(-1, 2, units, w_down.shape[1])
    down_mine = take(down_cut, 1, c).reshape(-1, w_down.shape[1])
    down_from = core_swap(take(down_cut, 1, 1 - c).reshape(-1, w_down.shape[1]))
    down_local = in_core_order(down_mine, down_from, 1).reshape(down_mine.shape[0], -1)
    down_own = put(jnp.zeros((nd,) + down_local.shape, BF), down_local[None], 0, d)
    for m in range(1, nd):
        down_own = put(down_own, dp_xor(down_local, m)[None], 0, d ^ m)
    down_own = down_own.reshape(-1, down_local.shape[1])
    down_own = [down_own] + [z_shift(down_own, s) for s in range(1, nz)]
    down_other = [core_swap(piece) for piece in down_own]

    lane = np.arange(128)
    frequency = jnp.power(theta_base, -jnp.asarray(lane % HALF, F32) * 2.0 / HEAD_SIZE)
    angle = positions.reshape(rows, 1).astype(F32) * frequency[None, :]
    cosine = jnp.cos(angle)
    sine = jnp.sin(angle) * jnp.asarray(np.where(lane % HEAD_SIZE < HALF, -1.0, 1.0), F32)[None, :]

    inputs = hidden_in.reshape(rows, width).astype(F32)
    scale_one = norm_scale(inputs)
    normed_one = (inputs * scale_one * gain_attn).astype(BF)
    one_blocks = to_blocks(normed_one, nd)
    kw = KEY_VALUE_HEADS * HEAD_SIZE
    kv_own = project(one_blocks, dp_index, kv_weights, BF, (cosine, sine), kw)
    query = project(one_blocks, dp_index, q_weights, BF, (cosine, sine), QUERY_HEADS * HEAD_SIZE)

    first_query = rank * span
    att_list, lse_list, kv_list, info_list, start_list = [], [], [], [], []
    for i in range(seqs):
        own = kv_own[i * span : (i + 1) * span][None, None]
        buffer = jnp.zeros((nz, 2, span, 2 * kw), BF)
        piece = own
        for s in range(nz):
            if s:
                piece = z_up(piece)
            place = (z - s) % nz
            buffer = lax.dynamic_update_slice(buffer, piece, (place, c, 0, 0))
            buffer = lax.dynamic_update_slice(buffer, core_swap(piece), (place, 1 - c, 0, 0))
        kv = buffer.reshape(length, 2 * kw)
        begin = (first_query + jnp.arange(span, dtype=jnp.int32) - positions[i]).reshape(span, 1)
        info = jnp.stack(
            [first_query, begin[0, 0] // block_size, (first_query + span - 1) // block_size + 1]
        ).astype(jnp.int32)
        att, lse = attend(info, begin, query[i * span : (i + 1) * span], kv, block_size)
        att_list.append(att)
        lse_list.append(lse)
        kv_list.append(kv)
        info_list.append(info)
        start_list.append(begin)
    attended = jnp.concatenate(att_list, axis=0)
    att_blocks = to_blocks(attended, nd)
    mid = inputs + project(att_blocks, dp_index, o_weights, F32)

    scale_two = norm_scale(mid)
    normed_two = (mid * scale_two * gain_ffn).astype(BF)
    two_blocks = to_blocks(normed_two, nd)
    top_grad = out_grad.reshape(rows, width)
    top_blocks = to_blocks(top_grad, nz)
    out_other, dn_other, dgu_other, dd_other = feed_forward(
        two_blocks, top_blocks, dp_index, z_index, gu_other, down_other
    )
    out_own, dn_own, dgu_own, dd_own = feed_forward(
        two_blocks, top_blocks, dp_index, z_index, gu_own, down_own
    )
    layer_out = (mid + from_blocks(out_other + out_own)).astype(BF)
    grad_two = from_blocks(dn_other + dn_own)

    def add(*values):
        total = values[0].astype(F32)
        for value in values[1:]:
            total = total + value.astype(F32)
        return total

    def over_dp(value):
        return add(value[0], *[dp_xor(value[m], m) for m in range(1, nd)])

    def over_z(value, axis):
        return add(take(value, axis, z), *[z_shift(take(value, axis, (z + s) % nz), s) for s in range(1, nz)])

    dgu = add(dgu_own, core_swap(dgu_other)).astype(BF)
    dgu = over_dp(dgu).astype(BF)
    dgu = over_z(dgu.reshape(2, nz, -1, dgu.shape[-1]), 1)
    w_gate_grad, w_up_grad = dgu[0].T, dgu[1].T

    dd = add(dd_own, core_swap(dd_other)).astype(BF)
    dd = add(dd[0], *[z_shift(dd[s], -s) for s in range(1, nz)]).astype(BF)
    dd = dd.reshape(nd, -1, dd.shape[-1])
    dd = add(take(dd, 0, d), *[dp_xor(take(dd, 0, d ^ m), m) for m in range(1, nd)])
    dd = dd.reshape(dd.shape[0], 2, -1)
    dd_from = core_swap(take(dd, 1, 1 - c))
    dd = in_core_order(
        take(dd, 1, c).reshape(-1, units, dd.shape[-1]), dd_from.reshape(-1, units, dd.shape[-1]), 1
    )
    w_down_grad = dd.reshape(w_down.shape)

    weighted_two = grad_two * gain_ffn
    ffn_sum = jnp.sum(grad_two * mid * scale_two, axis=0)
    grad_mid = (
        top_grad.astype(F32)
        + scale_two * weighted_two
        - mid * (scale_two * scale_two * scale_two) * jnp.mean(weighted_two * mid, axis=-1, keepdims=True)
    )
    grad_att, do = project_back(grad_mid.astype(BF), att_blocks, dp_index, o_weights)
    grad_att = from_blocks(grad_att).astype(BF)

    def rows_of(value, parts):
        cut = value.reshape(nd, parts, nz, 2, -1, value.shape[-1])

        def half(which):
            return take(cut, 3, which).transpose(0, 2, 1, 3, 4).reshape(nd, nz, -1, value.shape[-1])

        return half(c), half(1 - c)

    do_mine, do_other = rows_of(do, 1)
    do = over_dp(add(do_mine, core_swap(do_other)).astype(BF)).astype(BF)
    w_out_grad = over_z(do, 0).T

    dq_list, dkv_list = [], []
    for i in range(seqs):
        here = slice(i * span, (i + 1) * span)
        dq, dkv = attend_back(
            info_list[i], start_list[i], query[here], kv_list[i], att_list[i], grad_att[here], lse_list[i],
            cosine[here], sine[here], block_size,
        )
        cut = dkv.reshape(nz, 2, span, 2 * kw)
        mine = add(take(cut, 1, c), core_swap(take(cut, 1, 1 - c))).astype(BF)
        total = take(mine, 0, z).astype(F32)
        for s in range(1, nz):
            total = total + z_down(take(mine, 0, (z - s) % nz), s).astype(F32)
        dq_list.append(dq)
        dkv_list.append(total)
    dq = jnp.concatenate(dq_list, axis=0)
    dkv = jnp.concatenate(dkv_list, axis=0)
    dk, dv = dkv[:, :kw], dkv[:, kw:]
    lane = np.arange(kw)
    swapped = jnp.where(lane % HEAD_SIZE < HALF, jnp.roll(dk, -HALF, 1), jnp.roll(dk, HALF, 1))
    cos_wide = jnp.tile(cosine[:, :HEAD_SIZE], (1, KEY_VALUE_HEADS))
    sin_wide = jnp.tile(sine[:, :HEAD_SIZE], (1, KEY_VALUE_HEADS))
    dkv = jnp.concatenate([dk * cos_wide - swapped * sin_wide, dv], axis=1).astype(BF)

    dq_one, dq_w = project_back(dq, one_blocks, dp_index, q_weights)
    dkv_one, dkv_w = project_back(dkv, one_blocks, dp_index, kv_weights)
    q_mine, q_other = rows_of(dq_w[:, : QUERY_HEADS * HEAD_SIZE], 1)
    kv_mine, kv_other = rows_of(dkv_w, 2)
    q_rows = q_mine.shape[2]
    dw = add(
        jnp.concatenate([q_mine, kv_mine], axis=2),
        core_swap(jnp.concatenate([q_other, kv_other], axis=2)),
    ).astype(BF)
    dw = over_z(over_dp(dw).astype(BF), 0)
    k_rows = (dw.shape[0] - q_rows) // 2
    w_query_grad = dw[:q_rows].T
    w_key_grad = dw[q_rows : q_rows + k_rows].T
    w_value_grad = dw[q_rows + k_rows :].T

    grad_one = from_blocks(dq_one + dkv_one)
    weighted_one = grad_one * gain_attn
    attn_sum = jnp.sum(grad_one * inputs * scale_one, axis=0)
    grad_input = (
        grad_mid
        + scale_one * weighted_one
        - inputs * (scale_one * scale_one * scale_one) * jnp.mean(weighted_one * inputs, axis=-1, keepdims=True)
    )
    gain_sums = lax.psum(jnp.stack([attn_sum, ffn_sum]), ("dp", "ctx"))
    gain_own = lax.dynamic_slice_in_dim(gain_sums, rank * (width // nc), width // nc, 1)
    return (
        layer_out.reshape(seqs, span, width),
        grad_input.astype(BF).reshape(seqs, span, width),
        gain_own[0],
        w_query_grad,
        w_key_grad,
        w_value_grad,
        w_out_grad,
        gain_own[1],
        w_gate_grad,
        w_up_grad,
        w_down_grad,
    )


def solution(mesh):
    placed = (
        P("dp", "ctx", None),
        P("dp", "ctx"),
        P("ctx"),
        P("dp", "ctx"),
        P("dp", "ctx"),
        P("dp", "ctx"),
        P("dp", "ctx"),
        P("ctx"),
        P("dp", "ctx"),
        P("dp", "ctx"),
        P("dp", "ctx"),
        P("dp", "ctx", None),
    )
    return jax.shard_map(
        on_device,
        mesh=mesh,
        in_specs=placed,
        out_specs=(
            P("dp", "ctx", None),
            P("dp", "ctx", None),
            P("ctx"),
            P("dp", "ctx"),
            P("dp", "ctx"),
            P("dp", "ctx"),
            P("dp", "ctx"),
            P("ctx"),
            P("dp", "ctx"),
            P("dp", "ctx"),
            P("dp", "ctx"),
        ),
        check_vma=False,
    )
```

```python
import functools

import jax
import jax.numpy as jnp
import numpy as np
from jax import lax
from jax.experimental import pallas as pl
from jax.experimental.layout import Layout, with_layout_constraint
from jax.experimental.pallas import tpu as pltpu
from jax.sharding import PartitionSpec as P

QUERY_HEADS = 15
KEY_VALUE_HEADS = 5
HEAD_SIZE = 64
GROUP = QUERY_HEADS // KEY_VALUE_HEADS
HALF = HEAD_SIZE // 2

epsilon = 1e-05
theta_base = 100000.0
masked_score = -1e30
lowest_top = -1e29
score_scale = 0.125
VMEM_BYTES = 56 * 1024 * 1024

BF = jnp.bfloat16
F32 = jnp.float32


def dot_nn(a, b):
    return lax.dot_general(a, b, (((1,), (0,)), ((), ())), preferred_element_type=F32)


def dot_nt(a, b):
    return lax.dot_general(a, b, (((1,), (1,)), ((), ())), preferred_element_type=F32)


def dot_tn(a, b):
    return lax.dot_general(a, b, (((0,), (0,)), ((), ())), preferred_element_type=F32)


def vmem_spec():
    return pl.BlockSpec(memory_space=pltpu.VMEM)


def smem_spec():
    return pl.BlockSpec(memory_space=pltpu.SMEM)


def params():
    return pltpu.CompilerParams(vmem_limit_bytes=VMEM_BYTES)


def cost(flops, bytes_accessed, transcendentals=0):
    part = 64
    return pl.CostEstimate(
        flops=int(flops) // part,
        bytes_accessed=int(bytes_accessed) // part,
        transcendentals=int(transcendentals) // part,
    )


def rotate(value, cosine, sine, limit=None):
    width = value.shape[1]
    lane = lax.broadcasted_iota(jnp.int32, value.shape, 1)
    ahead = pltpu.roll(value, width - HALF, 1)
    behind = pltpu.roll(value, HALF, 1)
    swapped = jnp.where(lane % HEAD_SIZE < HALF, ahead, behind)
    copies = width // 128
    cos_wide = jnp.concatenate([cosine] * copies, axis=1)
    sin_wide = jnp.concatenate([sine] * copies, axis=1)
    turned = value * cos_wide + swapped * sin_wide
    if limit is not None:
        turned = jnp.where(lane < limit, turned, value)
    return turned


def row_chunks(rows):
    size = min(128, rows)
    return [slice(start, start + size) for start in range(0, rows, size)]


def column_chunks(columns):
    return [slice(start, min(start + 256, columns)) for start in range(0, columns, 256)]


def scale_of(value):
    return lax.rsqrt(jnp.mean(value * value, axis=1, keepdims=True) + epsilon)


def call(body, operands, n_smem, outs, flops, scratch=()):
    moved = sum(o.size * o.dtype.itemsize for o in operands) + sum(
        int(np.prod(o.shape)) * o.dtype.itemsize for o in outs
    )
    return pl.pallas_call(
        body,
        out_shape=tuple(outs),
        in_specs=[smem_spec()] * n_smem + [vmem_spec()] * (len(operands) - n_smem),
        out_specs=tuple(vmem_spec() for _ in outs),
        scratch_shapes=list(scratch),
        compiler_params=params(),
        cost_estimate=cost(flops, moved),
    )(*operands)


def shape(dims, dtype):
    return jax.ShapeDtypeStruct(tuple(dims), dtype)


def block_product(x_ref, index_ref, weights, columns):
    total = None
    for m, weight in enumerate(weights):
        term = dot_nt(x_ref[index_ref[m]], weight[columns, :])
        total = term if total is None else total + term
    return total


def keys_values(hidden, gain, index, weights, cosine, sine):
    nd = len(weights)
    rows, width = hidden.shape
    depth = width // nd
    columns = weights[0].shape[0]
    turn = KEY_VALUE_HEADS * HEAD_SIZE

    def body(index_ref, hidden_ref, gain_ref, cos_ref, sin_ref, *rest):
        w, (blocks_ref, kv_ref) = rest[:nd], rest[nd:]
        for here in row_chunks(rows):
            x = hidden_ref[here, :].astype(F32)
            normed = (x * scale_of(x) * gain_ref[...]).astype(BF)
            for b in range(nd):
                blocks_ref[b, here, :] = normed[:, b * depth : (b + 1) * depth]
        for cols in column_chunks(columns):
            total = block_product(blocks_ref, index_ref, w, cols)
            if turn > cols.start:
                total = rotate(total, cos_ref[...], sin_ref[...], turn - cols.start if turn < cols.stop else None)
            kv_ref[:, cols] = total.astype(BF)

    return call(
        body,
        [index, hidden, gain, cosine, sine, *weights],
        1,
        [shape((nd, rows, depth), BF), shape((rows, columns), BF)],
        2 * rows * columns * width,
    )


def queries(blocks, index, weights, cosine, sine):
    nd, rows, depth = blocks.shape
    columns = weights[0].shape[0]

    def body(index_ref, blocks_ref, cos_ref, sin_ref, *rest):
        w, out_ref = rest[:nd], rest[nd]
        for cols in column_chunks(columns):
            total = block_product(blocks_ref, index_ref, w, cols)
            out_ref[:, cols] = rotate(total, cos_ref[...], sin_ref[...]).astype(BF)

    return call(
        body,
        [index, blocks, cosine, sine, *weights],
        1,
        [shape((rows, columns), BF)],
        2 * rows * columns * nd * depth,
    )[0]


def middle(att_parts, hidden, gain, index, weights):
    nd = len(weights)
    parts = len(att_parts)
    rows, width = hidden.shape
    depth = width // nd
    span = rows // parts

    def body(index_ref, hidden_ref, gain_ref, *rest):
        att, w = rest[:parts], rest[parts : parts + nd]
        att_ref, mid_ref, two_ref = rest[parts + nd :]
        for p in range(parts):
            for b in range(nd):
                att_ref[b, p * span : (p + 1) * span, :] = att[p][:, b * depth : (b + 1) * depth]
        for cols in column_chunks(width):
            mid_ref[:, cols] = hidden_ref[:, cols].astype(F32) + block_product(att_ref, index_ref, w, cols)
        for here in row_chunks(rows):
            x = mid_ref[here, :]
            normed = (x * scale_of(x) * gain_ref[...]).astype(BF)
            for b in range(nd):
                two_ref[b, here, :] = normed[:, b * depth : (b + 1) * depth]

    return call(
        body,
        [index, hidden, gain, *att_parts, *weights],
        1,
        [
            shape((nd, rows, depth), BF),
            shape((rows, width), F32),
            shape((nd, rows, depth), BF),
        ],
        2 * rows * width * width,
    )


def middle_back(mid, out_grad, gain, index, att_blocks, made, dn, weights):
    nd = len(weights)
    rows, width = mid.shape
    depth = width // nd

    def body(index_ref, mid_ref, grad_ref, gain_ref, att_ref, made_ref, dn_ref, *rest):
        w = rest[:nd]
        layer_ref, dmid_ref, datt_ref, dw_ref, sum_ref, low_ref, block_ref = rest[nd:]
        sums = jnp.zeros((1, width), F32)
        for here in row_chunks(rows):
            x = mid_ref[here, :]
            up = grad_ref[here, :].astype(F32)
            layer_ref[here, :] = (x + made_ref[here, :]).astype(BF)
            dn = jnp.concatenate([dn_ref[b, here, :] for b in range(nd)], axis=1)
            scale = scale_of(x)
            weighted = dn * gain_ref[...]
            sums += jnp.sum(dn * x * scale, axis=0, keepdims=True)
            inner = jnp.mean(weighted * x, axis=1, keepdims=True)
            dmid = up + scale * weighted - x * (scale * scale * scale * inner)
            dmid_ref[here, :] = dmid
            low_ref[here, :] = dmid.astype(BF)
        sum_ref[...] = sums
        for m in range(nd):
            place = index_ref[m]
            block_ref[place] = dot_nn(low_ref[...], w[m][...])
            for cols in column_chunks(width):
                dw_ref[m, cols, :] = dot_tn(low_ref[:, cols], att_ref[place]).astype(BF)
        for b in range(nd):
            datt_ref[:, b * depth : (b + 1) * depth] = block_ref[b].astype(BF)

    return call(
        body,
        [index, mid, out_grad, gain, att_blocks, made, dn, *weights],
        1,
        [
            shape((rows, width), BF),
            shape((rows, width), F32),
            shape((rows, width), BF),
            shape((nd, width, depth), BF),
            shape((1, width), F32),
        ],
        4 * rows * width * width,
        [pltpu.VMEM((rows, width), BF), pltpu.VMEM((nd, rows, depth), F32)],
    )


def queries_back(dq_parts, blocks, index, weights):
    nd, rows, depth = blocks.shape
    parts = len(dq_parts)
    span = rows // parts
    columns = weights[0].shape[0]

    def body(index_ref, blocks_ref, *rest):
        dq, w = rest[:parts], rest[parts : parts + nd]
        dx_ref, dw_ref, all_ref = rest[parts + nd :]
        for p in range(parts):
            all_ref[p * span : (p + 1) * span, :] = dq[p][...]
        for m in range(nd):
            place = index_ref[m]
            dx_ref[place] = dot_nn(all_ref[...], w[m][...])
            for cols in column_chunks(columns):
                dw_ref[m, cols, :] = dot_tn(all_ref[:, cols], blocks_ref[place]).astype(BF)

    return call(
        body,
        [index, blocks, *dq_parts, *weights],
        1,
        [shape((nd, rows, depth), F32), shape((nd, columns, depth), BF)],
        4 * rows * columns * nd * depth,
        [pltpu.VMEM((rows, columns), BF)],
    )


def keys_values_back(dkv_parts, blocks, dx_blocks, dmid, hidden, gain, index, weights, cosine, sine):
    nd, rows, depth = blocks.shape
    parts = len(dkv_parts)
    columns = weights[0].shape[0]
    width = nd * depth
    turn = KEY_VALUE_HEADS * HEAD_SIZE
    pieces = len(dkv_parts[0])
    flat = [piece for part in dkv_parts for piece in part]
    span = rows // parts

    def body(index_ref, blocks_ref, dx_ref, dmid_ref, hidden_ref, gain_ref, cos_ref, sin_ref, *rest):
        got, w = rest[: parts * pieces], rest[parts * pieces : parts * pieces + nd]
        grad_ref, dw_ref, sum_ref, low_ref, block_ref = rest[parts * pieces + nd :]
        for p in range(parts):
            here = slice(p * span, (p + 1) * span)
            for cols in column_chunks(columns):
                total = got[p * pieces][:, cols].astype(F32)
                for piece in got[p * pieces + 1 : (p + 1) * pieces]:
                    total = total + piece[:, cols].astype(F32)
                if turn > cols.start:
                    limit = turn - cols.start if turn < cols.stop else None
                    total = rotate(total, cos_ref[here, :], -sin_ref[here, :], limit)
                low_ref[here, cols] = total.astype(BF)
        for m in range(nd):
            place = index_ref[m]
            block_ref[place] = dx_ref[place] + dot_nn(low_ref[...], w[m][...])
            for cols in column_chunks(columns):
                dw_ref[m, cols, :] = dot_tn(low_ref[:, cols], blocks_ref[place]).astype(BF)
        sums = jnp.zeros((1, width), F32)
        for here in row_chunks(rows):
            x = hidden_ref[here, :].astype(F32)
            dn = jnp.concatenate([block_ref[b, here, :] for b in range(nd)], axis=1)
            scale = scale_of(x)
            weighted = dn * gain_ref[...]
            sums += jnp.sum(dn * x * scale, axis=0, keepdims=True)
            inner = jnp.mean(weighted * x, axis=1, keepdims=True)
            grad = dmid_ref[here, :] + scale * weighted - x * (scale * scale * scale * inner)
            grad_ref[here, :] = grad.astype(BF)
        sum_ref[...] = sums

    return call(
        body,
        [index, blocks, dx_blocks, dmid, hidden, gain, cosine, sine, *flat, *weights],
        1,
        [shape((rows, width), BF), shape((nd, columns, depth), BF), shape((1, width), F32)],
        4 * rows * columns * width,
        [pltpu.VMEM((rows, columns), BF), pltpu.VMEM((nd, rows, depth), F32)],
    )


def feed_forward(core, blocks, top, weights, part):
    nd, nz, _, _, depth = weights.shape
    wide = depth + -depth % 128
    rows, width = top.shape
    sub = nz // nd
    half = sub * part
    z_depth = width // nz

    def body(
        core_ref, n2_ref, top_ref, gu_own, gu_other, down_own, down_other, out_ref, dn_ref, dw_own, dw_other,
        tops, outs, w_gu, w_down, dgu, dd, sems,
    ):
        step = pl.program_id(0)

        def copies(at):
            made = []
            for h, ref in enumerate((dw_own, dw_other)):
                made.append(
                    pltpu.make_async_copy(
                        dgu.at[h], ref.at[:, pl.ds(at * sub, sub), pl.ds(0, 2)], sems.at[2 * h]
                    )
                )
                made.append(
                    pltpu.make_async_copy(dd.at[h], ref.at[at, :, pl.ds(2, 1)], sems.at[2 * h + 1])
                )
            return made

        @pl.when(step == 0)
        def _():
            dn_ref[...] = jnp.zeros_like(dn_ref)
            outs[...] = jnp.zeros_like(outs)
            dgu[...] = jnp.zeros_like(dgu)
            dd[...] = jnp.zeros_like(dd)
            for b in range(nz):
                tops[b] = top_ref[:, b * z_depth : (b + 1) * z_depth]

        for h, (gu, down) in enumerate(((gu_own, down_own), (gu_other, down_other))):
            here = slice(h * half, (h + 1) * half)
            for b in range(nd):
                for which in range(2):
                    w_gu[b, which, here, :] = gu[b, :, 0, which * part : (which + 1) * part].reshape(half, depth)
            for b in range(nz):
                for s in range(sub):
                    w_down[b, h * half + s * part : h * half + (s + 1) * part, :] = down[
                        0, b, 0, :, s * z_depth : (s + 1) * z_depth
                    ]

        gate = up = grad_hidden = None
        for b in range(nd):
            term_g = dot_nt(n2_ref[b], w_gu[b, 0])
            term_u = dot_nt(n2_ref[b], w_gu[b, 1])
            gate = term_g if gate is None else gate + term_g
            up = term_u if up is None else up + term_u
        for b in range(nz):
            term = dot_nt(tops[b], w_down[b])
            grad_hidden = term if grad_hidden is None else grad_hidden + term
        sig = jax.nn.sigmoid(gate)
        act = gate * sig
        hidden = (act * up).astype(BF)
        d_gate = (grad_hidden * up * sig * (1.0 + gate * (1.0 - sig))).astype(BF)
        d_up = (grad_hidden * act).astype(BF)

        @pl.when(step > 0)
        def _():
            for copy in copies(step - 1):
                copy.wait()

        for b in range(nz):
            outs[b] += dot_nn(hidden, w_down[b])
            grad = dot_tn(hidden, tops[b]).astype(BF)
            for h in range(2):
                for s in range(sub):
                    start = h * half + s * part
                    dd[h, b, 0, :, s * z_depth : (s + 1) * z_depth] = grad[start : start + part]
        for b in range(nd):
            dn_ref[b] += dot_nn(d_gate, w_gu[b, 0]) + dot_nn(d_up, w_gu[b, 1])
            for which, value in ((0, d_gate), (1, d_up)):
                grad = dot_tn(value, n2_ref[b]).astype(BF)
                for h in range(2):
                    dgu[h, b, :, which, :, :depth] = grad[h * half : (h + 1) * half].reshape(sub, part, depth)
        for copy in copies(step):
            copy.start()

        @pl.when(step == nd - 1)
        def _():
            for b in range(nz):
                out_ref[:, b * z_depth : (b + 1) * z_depth] = outs[b]
            for copy in copies(step):
                copy.wait()

    def gu_spec(other):
        return pl.BlockSpec(
            (nd, sub, 1, 2 * part, depth),
            lambda i, core: (0, i, 1 - core[0] if other else core[0], 0, 0),
        )

    def down_spec(other):
        return pl.BlockSpec(
            (1, nz, 1, part, depth),
            lambda i, core: (i, 0, 1 - core[0] if other else core[0], 2, 0),
        )

    grad = shape((nd, nz, 3, part, wide), BF)
    return pl.pallas_call(
        body,
        grid_spec=pltpu.PrefetchScalarGridSpec(
            num_scalar_prefetch=1,
            grid=(nd,),
            in_specs=[
                pl.BlockSpec(blocks.shape, lambda i, core: (0, 0, 0)),
                pl.BlockSpec(top.shape, lambda i, core: (0, 0)),
                gu_spec(False),
                gu_spec(True),
                down_spec(False),
                down_spec(True),
            ],
            out_specs=(
                pl.BlockSpec((rows, width), lambda i, core: (0, 0)),
                pl.BlockSpec(blocks.shape, lambda i, core: (0, 0, 0)),
                pl.BlockSpec(memory_space=pl.ANY),
                pl.BlockSpec(memory_space=pl.ANY),
            ),
            scratch_shapes=[
                pltpu.VMEM((nz, rows, z_depth), BF),
                pltpu.VMEM((nz, rows, z_depth), F32),
                pltpu.VMEM((nd, 2, 2 * half, depth), BF),
                pltpu.VMEM((nz, 2 * half, z_depth), BF),
                pltpu.VMEM((2, nd, sub, 2, part, wide), BF),
                pltpu.VMEM((2, nz, 1, part, wide), BF),
                pltpu.SemaphoreType.DMA((4,)),
            ],
        ),
        out_shape=(shape((rows, width), F32), shape(blocks.shape, F32), grad, grad),
        compiler_params=params(),
        cost_estimate=cost(36 * rows * half * nd * width, 24 * half * nd * width, 2 * rows * half * nd),
    )(core, blocks, top, weights, weights, weights, weights)


def group_rows(ref, g):
    return jnp.concatenate(
        [ref[:, (g * GROUP + i) * HEAD_SIZE : (g * GROUP + i + 1) * HEAD_SIZE] for i in range(GROUP)],
        axis=0,
    )


def bias_of(start_ref, first_query, first_key, span, size):
    key = first_key + lax.broadcasted_iota(jnp.int32, (size, span), 0)
    query = first_query + lax.broadcasted_iota(jnp.int32, (size, span), 1)
    allowed = (key <= query) & (key >= start_ref[...])
    return jnp.concatenate([jnp.where(allowed, 0.0, masked_score)] * GROUP, axis=1)


def attend_kernel(
    span, size, pieces, info_ref, start_ref, q_ref, own, other, kv_ref, att_ref, lse_ref, acc, top, total, q_rows
):
    first_query = info_ref[0]
    for s in range(pieces):
        place = info_ref[4 + s]
        for ref, core in ((own, info_ref[3]), (other, 1 - info_ref[3])):
            kv_ref[pl.ds(pl.multiple_of((2 * place + core) * span, span), span), :] = ref[s]
    top[...] = jnp.full_like(top, lowest_top)
    total[...] = jnp.zeros_like(total)
    acc[...] = jnp.zeros_like(acc)
    value_at = KEY_VALUE_HEADS * HEAD_SIZE
    for g in range(KEY_VALUE_HEADS):
        q_rows[g] = group_rows(q_ref, g) * BF(score_scale)

    def one_block(block, carry):
        first_key = pl.multiple_of(block * size, size)
        bias = bias_of(start_ref, first_query, first_key, span, size)
        for g in range(KEY_VALUE_HEADS):
            k_at, v_at = g * HEAD_SIZE, value_at + g * HEAD_SIZE
            keys = kv_ref[pl.ds(first_key, size), k_at : k_at + HEAD_SIZE]
            values = kv_ref[pl.ds(first_key, size), v_at : v_at + HEAD_SIZE]
            scores = dot_nt(keys, q_rows[g]) + bias
            old_top = top[g]
            new_top = jnp.maximum(old_top, jnp.max(scores, axis=0, keepdims=True))
            rescale = jnp.exp(old_top - new_top)
            expo = jnp.exp(scores - new_top)
            total[g] = total[g] * rescale + jnp.sum(expo, axis=0, keepdims=True)
            acc[g] = acc[g] * rescale + dot_tn(values, expo.astype(BF))
            top[g] = new_top
        return carry

    lax.fori_loop(info_ref[1], info_ref[2], one_block, 0)
    for g in range(KEY_VALUE_HEADS):
        whole = total[g]
        result = (acc[g] * (1.0 / whole)).T.astype(BF)
        lse_ref[g] = top[g] + jnp.log(whole)
        for i in range(GROUP):
            h = g * GROUP + i
            att_ref[:, h * HEAD_SIZE : (h + 1) * HEAD_SIZE] = result[i * span : (i + 1) * span]


def attend(info, start, q, own, other, size):
    span = q.shape[0]
    rows = GROUP * span
    pieces = own.shape[0]
    length = 2 * pieces * span
    return pl.pallas_call(
        functools.partial(attend_kernel, span, size, pieces),
        out_shape=(
            jax.ShapeDtypeStruct((length, 2 * KEY_VALUE_HEADS * HEAD_SIZE), BF),
            jax.ShapeDtypeStruct((span, QUERY_HEADS * HEAD_SIZE), BF),
            jax.ShapeDtypeStruct((KEY_VALUE_HEADS, 1, rows), F32),
        ),
        in_specs=[smem_spec()] + [vmem_spec()] * 4,
        out_specs=(vmem_spec(), vmem_spec(), vmem_spec()),
        scratch_shapes=[
            pltpu.VMEM((KEY_VALUE_HEADS, HEAD_SIZE, rows), F32),
            pltpu.VMEM((KEY_VALUE_HEADS, 1, rows), F32),
            pltpu.VMEM((KEY_VALUE_HEADS, 1, rows), F32),
            pltpu.VMEM((KEY_VALUE_HEADS, rows, HEAD_SIZE), BF),
        ],
        compiler_params=params(),
        cost_estimate=cost(
            16 * QUERY_HEADS * HEAD_SIZE * span * length,
            4 * length * KEY_VALUE_HEADS * HEAD_SIZE,
            QUERY_HEADS * span * length,
        ),
    )(info, start, q, own, other)


def attend_back_kernel(
    span, size, info_ref, start_ref, q_ref, kv_ref, att_ref, datt_ref, lse_ref, cos_ref, sin_ref,
    dq_ref, dkv_ref, dq_acc, q_rows, d_rows, dot_rows,
):
    first_query = info_ref[0]
    value_at = KEY_VALUE_HEADS * HEAD_SIZE
    dq_acc[...] = jnp.zeros_like(dq_acc)
    dkv_ref[...] = jnp.zeros_like(dkv_ref)
    for g in range(KEY_VALUE_HEADS):
        grads = group_rows(datt_ref, g)
        q_rows[g] = group_rows(q_ref, g) * BF(score_scale)
        d_rows[g] = grads
        products = grads.astype(F32) * group_rows(att_ref, g).astype(F32)
        dot_rows[g] = jnp.sum(products.T, axis=0, keepdims=True)

    def one_block(block, carry):
        first_key = pl.multiple_of(block * size, size)
        bias = bias_of(start_ref, first_query, first_key, span, size)
        for g in range(KEY_VALUE_HEADS):
            k_at, v_at = g * HEAD_SIZE, value_at + g * HEAD_SIZE
            rows = q_rows[g]
            grads = d_rows[g]
            keys = kv_ref[pl.ds(first_key, size), k_at : k_at + HEAD_SIZE]
            values = kv_ref[pl.ds(first_key, size), v_at : v_at + HEAD_SIZE]
            probs = jnp.exp((dot_nt(keys, rows) + bias) - lse_ref[g])
            d_probs = dot_nt(values, grads)
            d_scores = (probs * (d_probs - dot_rows[g])).astype(BF)
            dkv_ref[pl.ds(first_key, size), v_at : v_at + HEAD_SIZE] = dot_nn(
                probs.astype(BF), grads
            ).astype(BF)
            dkv_ref[pl.ds(first_key, size), k_at : k_at + HEAD_SIZE] = dot_nn(d_scores, rows).astype(BF)
            dq_acc[g] += dot_tn(keys, d_scores)
        return carry

    lax.fori_loop(info_ref[1], info_ref[2], one_block, 0)
    cosine, sine = cos_ref[...], -sin_ref[...]
    for start in range(0, QUERY_HEADS + 1, 2):
        parts = []
        for h in (start, start + 1):
            if h < QUERY_HEADS:
                g, i = h // GROUP, h % GROUP
                parts.append(dq_acc[g, :, i * span : (i + 1) * span] * score_scale)
            else:
                parts.append(jnp.zeros((HEAD_SIZE, span), F32))
        pair = jnp.concatenate(parts, axis=0).T
        dq_ref[:, start * HEAD_SIZE : (start + 2) * HEAD_SIZE] = rotate(pair, cosine, sine).astype(BF)


def attend_back(info, start, q, kv, att, datt, lse, cosine, sine, size):
    span = q.shape[0]
    rows = GROUP * span
    length = kv.shape[0]
    per_head = (KEY_VALUE_HEADS, rows, HEAD_SIZE)
    per_row = (KEY_VALUE_HEADS, 1, rows)
    return pl.pallas_call(
        functools.partial(attend_back_kernel, span, size),
        out_shape=(
            jax.ShapeDtypeStruct((span, q.shape[1]), BF),
            jax.ShapeDtypeStruct(kv.shape, BF),
        ),
        in_specs=[smem_spec()] + [vmem_spec()] * 8,
        out_specs=(vmem_spec(), vmem_spec()),
        scratch_shapes=[
            pltpu.VMEM((KEY_VALUE_HEADS, HEAD_SIZE, rows), F32),
            pltpu.VMEM(per_head, BF),
            pltpu.VMEM(per_head, BF),
            pltpu.VMEM(per_row, F32),
        ],
        compiler_params=params(),
        cost_estimate=cost(
            40 * QUERY_HEADS * HEAD_SIZE * span * length,
            8 * length * KEY_VALUE_HEADS * HEAD_SIZE,
            QUERY_HEADS * span * length,
        ),
    )(info, start, q, kv, att, datt, lse, cosine, sine)


def in_rows(value):
    return with_layout_constraint(value, Layout(tuple(range(value.ndim))))


def after(value, *others):
    return lax.optimization_barrier((value, *others))[0]


def on_device(
    hidden_in,
    positions,
    attn_gain,
    w_query,
    key_projection_weight,
    w_value,
    w_out,
    ffn_gain,
    w_gate,
    w_up,
    w_down,
    out_grad,
):
    nd, nz = lax.axis_size("dp"), lax.axis_size("z")
    nc = 2 * nz
    seqs, span, width = hidden_in.shape
    rows = seqs * span
    length = span * nc
    d, z, c = lax.axis_index("dp"), lax.axis_index("z"), lax.axis_index("core")
    rank = 2 * z + c
    first = c == 0
    block_size = min(512, length)

    def send(value, to):
        pairs = []
        for di in range(nd):
            for zi in range(nz):
                for ci in range(2):
                    target = to(di, zi, ci)
                    if target is not None:
                        dt, zt, ct = target
                        pairs.append((di * nc + zi * 2 + ci, dt * nc + zt * 2 + ct))
        return lax.ppermute(value, ("dp", "z", "core"), pairs)

    def z_shift(value, s):
        return send(value, lambda di, zi, ci: (di, (zi + s) % nz, ci))

    def z_up(value, s):
        return send(value, lambda di, zi, ci: (di, zi + s, ci) if zi + s < nz else None)

    def z_down(value, s):
        return send(value, lambda di, zi, ci: (di, zi - s, ci) if zi >= s else None)

    def dp_xor(value, m):
        return send(value, lambda di, zi, ci: (di ^ m, zi, ci))

    def core_swap(value):
        return send(value, lambda di, zi, ci: (di, zi, 1 - ci))

    def put(buffer, piece, axis, place):
        return lax.dynamic_update_slice_in_dim(buffer, piece, place, axis)

    def take(value, axis, place):
        return lax.dynamic_index_in_dim(value, place, axis, keepdims=False)

    def in_core_order(own, other, axis):
        return jnp.stack([jnp.where(first, own, other), jnp.where(first, other, own)], axis=axis)

    dp_index = jnp.bitwise_xor(d, jnp.arange(nd, dtype=jnp.int32))
    z_index = (z - jnp.arange(nz, dtype=jnp.int32)) % nz

    def pair(left, right):
        return in_rows(jnp.stack([left.T, right.T]))

    dl = w_query.shape[0]
    own_rows = key_projection_weight.shape[1]
    early = 2 * own_rows + 8
    gain_row = jnp.concatenate([attn_gain, ffn_gain])[None]
    gain_row = jnp.pad(gain_row, ((0, 7), (0, dl - gain_row.shape[1])))
    local = [pair(key_projection_weight, w_value).reshape(-1, dl), gain_row, in_rows(w_query.T)]
    kvq_z = lax.all_gather(in_rows(jnp.concatenate(local)), "z")
    kv_own = lax.all_gather(in_rows(kvq_z[:, :early]), "dp")
    q_z = in_rows(kvq_z[:, early:])
    q_own = [q_z] + [dp_xor(after(q_z, kv_own), m) for m in range(1, nd)]
    both = in_core_order(kv_own, core_swap(kv_own), 2)
    kv_weights = both[:, :, :, : 2 * own_rows].reshape(nd, nc, 2, own_rows, dl).swapaxes(1, 2)
    kv_weights = [in_rows(take(kv_weights, 0, d ^ m).reshape(-1, dl)) for m in range(nd)]
    gains = both[0, :, :, 2 * own_rows, : 2 * (width // nc)].reshape(nc, 2, -1).swapaxes(0, 1)
    gains = gains.reshape(2, 1, width).astype(F32)
    gain_attn, gain_ffn = gains[0], gains[1]

    units = w_gate.shape[1]
    down_cut = w_down.reshape(-1, 2, units, w_down.shape[1])
    down_mine, down_away = take(down_cut, 1, c), take(down_cut, 1, 1 - c)
    down_local = in_core_order(down_mine, core_swap(down_away), 2).swapaxes(0, 1).reshape(1, units, dl)
    late_local = jnp.concatenate([pair(w_gate, w_up), down_local]).reshape(-1, dl)
    late_local = in_rows(jnp.concatenate([late_local, in_rows(w_out.T)]))
    late = lax.all_gather(late_local, ("dp", "z", "core")).reshape(nd, nz, 2, -1, dl)

    lane = np.arange(128)
    frequency = jnp.power(theta_base, -jnp.asarray(lane % HALF, F32) * 2.0 / HEAD_SIZE)
    angle = positions.reshape(rows, 1).astype(F32) * frequency[None, :]
    cosine = jnp.cos(angle)
    sine = jnp.sin(angle) * jnp.asarray(np.where(lane % HEAD_SIZE < HALF, -1.0, 1.0), F32)[None, :]

    hidden_rows = hidden_in.reshape(rows, width)
    top_grad = out_grad.reshape(rows, width)
    one_blocks, kv_here = keys_values(hidden_rows, gain_attn, dp_index, kv_weights, cosine, sine)

    first_query = rank * span
    kv_up = []
    for i in range(seqs):
        piece = kv_here[i * span : (i + 1) * span]
        if i:
            piece = after(piece, kv_up[-1][1])
        kv_up.append([piece] + [z_up(piece, s) for s in range(1, nz)])

    q_own = jnp.stack([after(piece, kv_here) for piece in q_own])
    q_weights = in_core_order(q_own, core_swap(q_own), 2).reshape(nd, -1, dl)
    padding = -(QUERY_HEADS * HEAD_SIZE) % 128
    q_weights = [in_rows(jnp.pad(q_weights[m], ((0, padding), (0, 0)))) for m in range(nd)]
    one_blocks = after(one_blocks, kv_up[0][1])
    query = queries(one_blocks, dp_index, q_weights, cosine, sine)
    att_list, lse_list, kv_list, info_list, start_list = [], [], [], [], []
    for i in range(seqs):
        begin = (first_query + jnp.arange(span, dtype=jnp.int32) - positions[i]).reshape(1, span)
        info = jnp.concatenate(
            [
                jnp.stack(
                    [first_query, begin[0, 0] // block_size, (first_query + span - 1) // block_size + 1, c]
                ),
                z_index,
            ]
        ).astype(jnp.int32)
        own = kv_up[i] if i == 0 else [after(piece, att_list[-1]) for piece in kv_up[i]]
        own = jnp.stack(own)
        kv, att, lse = attend(info, begin, query[i * span : (i + 1) * span], own, core_swap(own), block_size)
        att_list.append(att)
        lse_list.append(lse)
        kv_list.append(kv)
        info_list.append(info)
        start_list.append(begin)
    late = after(late, att_list[0])
    o_weights = late[:, :, :, 3 * units :].reshape(nd, width, dl)
    o_weights = [in_rows(take(o_weights, 0, d ^ m)) for m in range(nd)]
    att_blocks, mid, two_blocks = middle(att_list, hidden_rows, gain_ffn, dp_index, o_weights)

    made, dn, ffn_grad, ffn_away = feed_forward(
        c.reshape(1).astype(jnp.int32), two_blocks, top_grad, late, units
    )
    layer_out, grad_mid, grad_att, do, ffn_sum = middle_back(
        mid, top_grad, gain_ffn, dp_index, att_blocks, made, dn, o_weights
    )

    def add(*values):
        total = values[0].astype(F32)
        for value in values[1:]:
            total = total + value.astype(F32)
        return total

    def over_dp(value):
        return add(value[0], *[dp_xor(value[m], m) for m in range(1, nd)])

    def over_z(value, axis):
        return add(take(value, axis, z), *[z_shift(take(value, axis, (z + s) % nz), s) for s in range(1, nz)])

    def rows_of(value, parts):
        cut = value.reshape(nd, parts, nz, 2, -1, value.shape[-1])

        def half(which):
            return take(cut, 3, which).transpose(0, 2, 1, 3, 4).reshape(nd, nz, -1, value.shape[-1])

        return half(c), half(1 - c)

    def finish(value):
        return in_rows(over_z(value.reshape(nz, -1, value.shape[-1]), 0)).T

    ffn_grad = add(ffn_grad, after(core_swap(ffn_away), grad_att)).astype(BF)
    grad_att = after(grad_att, ffn_grad)
    ffn_grad = in_rows(ffn_grad.reshape(nd, -1, ffn_grad.shape[-1]))
    ffn_scattered = in_rows(lax.psum_scatter(ffn_grad, "dp", scatter_dimension=0, tiled=True))
    ffn_grad = over_z(ffn_scattered.reshape(nz, 3, units, -1), 0)
    ffn_grad = in_rows(ffn_grad[:, :, :dl])
    w_gate_grad, w_up_grad = ffn_grad[0].T, ffn_grad[1].T
    down_cut = ffn_grad[2].reshape(units, -1, 2, w_down.shape[1]).swapaxes(0, 1)
    down_from = core_swap(take(down_cut, 2, 1 - c))
    w_down_grad = in_core_order(take(down_cut, 2, c), down_from, 1).reshape(w_down.shape)

    dq_list, dkv_list = [], []
    for i in range(seqs):
        here = slice(i * span, (i + 1) * span)
        grad_here = grad_att[here]
        if i:
            grad_here = after(grad_here, mine)
        dq, dkv = attend_back(
            info_list[i], start_list[i], query[here], kv_list[i], att_list[i], grad_here, lse_list[i],
            cosine[here], sine[here], block_size,
        )
        if i:
            dkv = after(dkv, *dkv_list[-1])
        cut = dkv.reshape(nz, 2, span, dkv.shape[-1])
        mine = add(take(cut, 1, c), core_swap(take(cut, 1, 1 - c))).astype(BF)
        dkv_list.append(
            [take(mine, 0, z)] + [z_down(take(mine, 0, (z - s) % nz), s) for s in range(1, nz)]
        )
        dq_list.append(dq)
    dx_blocks, dq_w = queries_back([after(dq, mine) for dq in dq_list], one_blocks, dp_index, q_weights)
    do_mine, do_other = rows_of(do, 1)
    q_mine, q_other = rows_of(dq_w[:, : QUERY_HEADS * HEAD_SIZE], 1)
    dqo = core_swap(after(jnp.concatenate([q_other, do_other], axis=2), *dkv_list[-1]))
    dqo = add(jnp.concatenate([q_mine, do_mine], axis=2), dqo).astype(BF)
    dqo = finish(over_dp(dqo).astype(BF))
    w_query_grad, w_out_grad = jnp.split(dqo, 2, axis=1)

    input_grad, dkv_w, attn_sum = keys_values_back(
        dkv_list, one_blocks, dx_blocks, grad_mid, hidden_rows, gain_attn, dp_index, kv_weights, cosine, sine
    )
    kv_mine, kv_other = rows_of(dkv_w, 2)
    sums = jnp.concatenate([attn_sum, ffn_sum]).reshape(2, nz, 2, -1).transpose(2, 1, 0, 3).reshape(2, nz, 1, -1)
    sums = jnp.pad(sums, ((0, 0), (0, 0), (0, 7), (0, dl - sums.shape[3]))).astype(BF)

    def with_sums(value, which):
        more = jnp.broadcast_to(take(sums, 0, which)[None], (nd,) + sums.shape[1:])
        return jnp.concatenate([value, more], axis=2)

    dkv_from = after(core_swap(with_sums(kv_other, 1 - c)), ffn_scattered)
    dkv_w = add(with_sums(kv_mine, c), dkv_from).astype(BF)
    dkv_w = in_rows(over_z(over_dp(dkv_w).astype(BF), 0))
    w_key_grad, w_value_grad = dkv_w[:own_rows].T, dkv_w[own_rows : 2 * own_rows].T
    gain_own = dkv_w[2 * own_rows, : 2 * (width // nc)].reshape(2, -1)
    return (
        layer_out.reshape(seqs, span, width),
        input_grad.reshape(seqs, span, width),
        gain_own[0],
        w_query_grad,
        w_key_grad,
        w_value_grad,
        w_out_grad,
        gain_own[1],
        w_gate_grad,
        w_up_grad,
        w_down_grad,
    )


def solution(mesh):
    mesh = jax.sharding.Mesh(
        mesh.devices.reshape(mesh.shape["dp"], mesh.shape["ctx"] // 2, 2), ("dp", "z", "core")
    )
    placed = (
        P("dp", ("z", "core"), None),
        P("dp", ("z", "core")),
        P(("z", "core")),
        P("dp", ("z", "core")),
        P("dp", ("z", "core")),
        P("dp", ("z", "core")),
        P("dp", ("z", "core")),
        P(("z", "core")),
        P("dp", ("z", "core")),
        P("dp", ("z", "core")),
        P("dp", ("z", "core")),
        P("dp", ("z", "core"), None),
    )
    return jax.shard_map(
        on_device,
        mesh=mesh,
        in_specs=placed,
        out_specs=(
            P("dp", ("z", "core"), None),
            P("dp", ("z", "core"), None),
            P(("z", "core")),
            P("dp", ("z", "core")),
            P("dp", ("z", "core")),
            P("dp", ("z", "core")),
            P("dp", ("z", "core")),
            P(("z", "core")),
            P("dp", ("z", "core")),
            P("dp", ("z", "core")),
            P("dp", ("z", "core")),
        ),
        check_vma=False,
    )
```

```python
import functools

import jax
import jax.numpy as jnp
import numpy as np
from jax import lax
from jax.experimental import pallas as pl
from jax.experimental.layout import Layout, with_layout_constraint
from jax.experimental.pallas import tpu as pltpu
from jax.sharding import PartitionSpec as P

QUERY_HEADS = 15
KEY_VALUE_HEADS = 5
HEAD_SIZE = 64
GROUP = QUERY_HEADS // KEY_VALUE_HEADS
HALF = HEAD_SIZE // 2

epsilon = 1e-05
theta_base = 100000.0
masked_score = -1e30
lowest_top = -1e29
score_scale = 0.125
VMEM_BYTES = 56 * 1024 * 1024

BF = jnp.bfloat16
F32 = jnp.float32


def dot_nn(a, b):
    return lax.dot_general(a, b, (((1,), (0,)), ((), ())), preferred_element_type=F32)


def dot_nt(a, b):
    return lax.dot_general(a, b, (((1,), (1,)), ((), ())), preferred_element_type=F32)


def dot_tn(a, b):
    return lax.dot_general(a, b, (((0,), (0,)), ((), ())), preferred_element_type=F32)


def vmem_spec():
    return pl.BlockSpec(memory_space=pltpu.VMEM)


def smem_spec():
    return pl.BlockSpec(memory_space=pltpu.SMEM)


def params():
    return pltpu.CompilerParams(vmem_limit_bytes=VMEM_BYTES)


def cost(flops, bytes_accessed, transcendentals=0):
    part = 64
    return pl.CostEstimate(
        flops=int(flops) // part,
        bytes_accessed=int(bytes_accessed) // part,
        transcendentals=int(transcendentals) // part,
    )


def rotate(value, cosine, sine, limit=None):
    width = value.shape[1]
    lane = lax.broadcasted_iota(jnp.int32, value.shape, 1)
    ahead = pltpu.roll(value, width - HALF, 1)
    behind = pltpu.roll(value, HALF, 1)
    swapped = jnp.where(lane % HEAD_SIZE < HALF, ahead, behind)
    copies = width // 128
    cos_wide = jnp.concatenate([cosine] * copies, axis=1)
    sin_wide = jnp.concatenate([sine] * copies, axis=1)
    turned = value * cos_wide + swapped * sin_wide
    if limit is not None:
        turned = jnp.where(lane < limit, turned, value)
    return turned


def row_chunks(rows):
    size = min(128, rows)
    return [slice(start, start + size) for start in range(0, rows, size)]


def column_chunks(columns):
    return [slice(start, min(start + 256, columns)) for start in range(0, columns, 256)]


def scale_of(value):
    return lax.rsqrt(jnp.mean(value * value, axis=1, keepdims=True) + epsilon)


def call(body, operands, n_smem, outs, flops, scratch=()):
    moved = sum(o.size * o.dtype.itemsize for o in operands) + sum(
        int(np.prod(o.shape)) * o.dtype.itemsize for o in outs
    )
    return pl.pallas_call(
        body,
        out_shape=tuple(outs),
        in_specs=[smem_spec()] * n_smem + [vmem_spec()] * (len(operands) - n_smem),
        out_specs=tuple(vmem_spec() for _ in outs),
        scratch_shapes=list(scratch),
        compiler_params=params(),
        cost_estimate=cost(flops, moved),
    )(*operands)


def shape(dims, dtype):
    return jax.ShapeDtypeStruct(tuple(dims), dtype)


def block_product(x_ref, index_ref, weights, columns):
    total = None
    for m, weight in enumerate(weights):
        term = dot_nt(x_ref[index_ref[m]], weight[columns, :])
        total = term if total is None else total + term
    return total


def keys_values(hidden, gain, index, weights, cosine, sine):
    nd = len(weights)
    rows, width = hidden.shape
    depth = width // nd
    columns = weights[0].shape[0]
    turn = KEY_VALUE_HEADS * HEAD_SIZE

    def body(index_ref, hidden_ref, gain_ref, cos_ref, sin_ref, *rest):
        w, (blocks_ref, kv_ref) = rest[:nd], rest[nd:]
        for here in row_chunks(rows):
            x = hidden_ref[here, :].astype(F32)
            normed = (x * scale_of(x) * gain_ref[...]).astype(BF)
            for b in range(nd):
                blocks_ref[b, here, :] = normed[:, b * depth : (b + 1) * depth]
        for cols in column_chunks(columns):
            total = block_product(blocks_ref, index_ref, w, cols)
            if turn > cols.start:
                total = rotate(total, cos_ref[...], sin_ref[...], turn - cols.start if turn < cols.stop else None)
            kv_ref[:, cols] = total.astype(BF)

    return call(
        body,
        [index, hidden, gain, cosine, sine, *weights],
        1,
        [shape((nd, rows, depth), BF), shape((rows, columns), BF)],
        2 * rows * columns * width,
    )


def queries(blocks, index, weights, cosine, sine):
    nd, rows, depth = blocks.shape
    columns = weights[0].shape[0]

    def body(index_ref, blocks_ref, cos_ref, sin_ref, *rest):
        w, out_ref = rest[:nd], rest[nd]
        for cols in column_chunks(columns):
            total = block_product(blocks_ref, index_ref, w, cols)
            out_ref[:, cols] = rotate(total, cos_ref[...], sin_ref[...]).astype(BF)

    return call(
        body,
        [index, blocks, cosine, sine, *weights],
        1,
        [shape((rows, columns), BF)],
        2 * rows * columns * nd * depth,
    )[0]


def middle(att_parts, hidden, gain, index, weights):
    nd = len(weights)
    parts = len(att_parts)
    rows, width = hidden.shape
    depth = width // nd
    span = rows // parts

    def body(index_ref, hidden_ref, gain_ref, *rest):
        att, w = rest[:parts], rest[parts : parts + nd]
        att_ref, mid_ref, two_ref = rest[parts + nd :]
        for p in range(parts):
            for b in range(nd):
                att_ref[b, p * span : (p + 1) * span, :] = att[p][:, b * depth : (b + 1) * depth]
        for cols in column_chunks(width):
            mid_ref[:, cols] = hidden_ref[:, cols].astype(F32) + block_product(att_ref, index_ref, w, cols)
        for here in row_chunks(rows):
            x = mid_ref[here, :]
            normed = (x * scale_of(x) * gain_ref[...]).astype(BF)
            for b in range(nd):
                two_ref[b, here, :] = normed[:, b * depth : (b + 1) * depth]

    return call(
        body,
        [index, hidden, gain, *att_parts, *weights],
        1,
        [
            shape((nd, rows, depth), BF),
            shape((rows, width), F32),
            shape((nd, rows, depth), BF),
        ],
        2 * rows * width * width,
    )


def middle_back(mid, out_grad, gain, index, att_blocks, made, dn, weights):
    nd = len(weights)
    rows, width = mid.shape
    depth = width // nd

    def body(index_ref, mid_ref, grad_ref, gain_ref, att_ref, made_ref, dn_ref, *rest):
        w = rest[:nd]
        layer_ref, dmid_ref, datt_ref, dw_ref, sum_ref, low_ref, block_ref = rest[nd:]
        sums = jnp.zeros((1, width), F32)
        for here in row_chunks(rows):
            x = mid_ref[here, :]
            up = grad_ref[here, :].astype(F32)
            layer_ref[here, :] = (x + made_ref[here, :]).astype(BF)
            dn = jnp.concatenate([dn_ref[b, here, :] for b in range(nd)], axis=1)
            scale = scale_of(x)
            weighted = dn * gain_ref[...]
            sums += jnp.sum(dn * x * scale, axis=0, keepdims=True)
            inner = jnp.mean(weighted * x, axis=1, keepdims=True)
            dmid = up + scale * weighted - x * (scale * scale * scale * inner)
            dmid_ref[here, :] = dmid
            low_ref[here, :] = dmid.astype(BF)
        sum_ref[...] = sums
        for m in range(nd):
            block_ref[index_ref[m]] = dot_nn(low_ref[...], w[m][...])
        for cols in column_chunks(width):
            turned = low_ref[:, cols].T
            for m in range(nd):
                dw_ref[m, cols, :] = dot_nn(turned, att_ref[index_ref[m]]).astype(BF)
        for b in range(nd):
            datt_ref[:, b * depth : (b + 1) * depth] = block_ref[b].astype(BF)

    return call(
        body,
        [index, mid, out_grad, gain, att_blocks, made, dn, *weights],
        1,
        [
            shape((rows, width), BF),
            shape((rows, width), F32),
            shape((rows, width), BF),
            shape((nd, width, depth), BF),
            shape((1, width), F32),
        ],
        4 * rows * width * width,
        [pltpu.VMEM((rows, width), BF), pltpu.VMEM((nd, rows, depth), F32)],
    )


def queries_back(dq_parts, blocks, index, weights):
    nd, rows, depth = blocks.shape
    parts = len(dq_parts)
    span = rows // parts
    columns = weights[0].shape[0]

    def body(index_ref, blocks_ref, *rest):
        dq, w = rest[:parts], rest[parts : parts + nd]
        dx_ref, dw_ref, all_ref = rest[parts + nd :]
        for p in range(parts):
            all_ref[p * span : (p + 1) * span, :] = dq[p][...]
        for m in range(nd):
            dx_ref[index_ref[m]] = dot_nn(all_ref[...], w[m][...])
        for cols in column_chunks(columns):
            turned = all_ref[:, cols].T
            for m in range(nd):
                dw_ref[m, cols, :] = dot_nn(turned, blocks_ref[index_ref[m]]).astype(BF)

    return call(
        body,
        [index, blocks, *dq_parts, *weights],
        1,
        [shape((nd, rows, depth), F32), shape((nd, columns, depth), BF)],
        4 * rows * columns * nd * depth,
        [pltpu.VMEM((rows, columns), BF)],
    )


def keys_values_back(dkv_parts, blocks, dx_blocks, dmid, hidden, gain, index, weights, cosine, sine):
    nd, rows, depth = blocks.shape
    parts = len(dkv_parts)
    columns = weights[0].shape[0]
    width = nd * depth
    turn = KEY_VALUE_HEADS * HEAD_SIZE
    pieces = len(dkv_parts[0])
    flat = [piece for part in dkv_parts for piece in part]
    span = rows // parts

    def body(index_ref, blocks_ref, dx_ref, dmid_ref, hidden_ref, gain_ref, cos_ref, sin_ref, *rest):
        got, w = rest[: parts * pieces], rest[parts * pieces : parts * pieces + nd]
        grad_ref, dw_ref, sum_ref, low_ref, block_ref = rest[parts * pieces + nd :]
        for p in range(parts):
            here = slice(p * span, (p + 1) * span)
            for cols in column_chunks(columns):
                total = got[p * pieces][:, cols].astype(F32)
                for piece in got[p * pieces + 1 : (p + 1) * pieces]:
                    total = total + piece[:, cols].astype(F32)
                if turn > cols.start:
                    limit = turn - cols.start if turn < cols.stop else None
                    total = rotate(total, cos_ref[here, :], -sin_ref[here, :], limit)
                low_ref[here, cols] = total.astype(BF)
        for m in range(nd):
            place = index_ref[m]
            block_ref[place] = dx_ref[place] + dot_nn(low_ref[...], w[m][...])
        for cols in column_chunks(columns):
            turned = low_ref[:, cols].T
            for m in range(nd):
                dw_ref[m, cols, :] = dot_nn(turned, blocks_ref[index_ref[m]]).astype(BF)
        sums = jnp.zeros((1, width), F32)
        for here in row_chunks(rows):
            x = hidden_ref[here, :].astype(F32)
            dn = jnp.concatenate([block_ref[b, here, :] for b in range(nd)], axis=1)
            scale = scale_of(x)
            weighted = dn * gain_ref[...]
            sums += jnp.sum(dn * x * scale, axis=0, keepdims=True)
            inner = jnp.mean(weighted * x, axis=1, keepdims=True)
            grad = dmid_ref[here, :] + scale * weighted - x * (scale * scale * scale * inner)
            grad_ref[here, :] = grad.astype(BF)
        sum_ref[...] = sums

    return call(
        body,
        [index, blocks, dx_blocks, dmid, hidden, gain, cosine, sine, *flat, *weights],
        1,
        [shape((rows, width), BF), shape((nd, columns, depth), BF), shape((1, width), F32)],
        4 * rows * columns * width,
        [pltpu.VMEM((rows, columns), BF), pltpu.VMEM((nd, rows, depth), F32)],
    )


def feed_forward(core, blocks, top, weights, part):
    nd, nz, _, _, depth = weights.shape
    wide = depth + -depth % 128
    rows, width = top.shape
    sub = nz // nd
    half = sub * part
    z_depth = width // nz

    def body(
        core_ref, n2_ref, top_ref, gu_own, gu_other, down_own, down_other, out_ref, dn_ref, dw_own, dw_other,
        tops, outs, w_gu, w_down, dgu, dd, sems,
    ):
        step = pl.program_id(0)

        def copies(at):
            made = []
            for h, ref in enumerate((dw_own, dw_other)):
                made.append(
                    pltpu.make_async_copy(
                        dgu.at[h], ref.at[:, pl.ds(at * sub, sub), pl.ds(0, 2)], sems.at[2 * h]
                    )
                )
                made.append(
                    pltpu.make_async_copy(dd.at[h], ref.at[at, :, pl.ds(2, 1)], sems.at[2 * h + 1])
                )
            return made

        @pl.when(step == 0)
        def _():
            dn_ref[...] = jnp.zeros_like(dn_ref)
            outs[...] = jnp.zeros_like(outs)
            dgu[...] = jnp.zeros_like(dgu)
            dd[...] = jnp.zeros_like(dd)
            for b in range(nz):
                tops[b] = top_ref[:, b * z_depth : (b + 1) * z_depth]

        for h, (gu, down) in enumerate(((gu_own, down_own), (gu_other, down_other))):
            here = slice(h * half, (h + 1) * half)
            for b in range(nd):
                for which in range(2):
                    w_gu[b, which, here, :] = gu[b, :, 0, which * part : (which + 1) * part].reshape(half, depth)
            for b in range(nz):
                for s in range(sub):
                    w_down[b, h * half + s * part : h * half + (s + 1) * part, :] = down[
                        0, b, 0, :, s * z_depth : (s + 1) * z_depth
                    ]

        gate = up = grad_hidden = None
        for b in range(nd):
            term_g = dot_nt(n2_ref[b], w_gu[b, 0])
            term_u = dot_nt(n2_ref[b], w_gu[b, 1])
            gate = term_g if gate is None else gate + term_g
            up = term_u if up is None else up + term_u
        for b in range(nz):
            term = dot_nt(tops[b], w_down[b])
            grad_hidden = term if grad_hidden is None else grad_hidden + term
        sig = jax.nn.sigmoid(gate)
        act = gate * sig
        hidden = (act * up).astype(BF)
        d_gate = (grad_hidden * up * sig * (1.0 + gate * (1.0 - sig))).astype(BF)
        d_up = (grad_hidden * act).astype(BF)

        @pl.when(step > 0)
        def _():
            for copy in copies(step - 1):
                copy.wait()

        hidden_t, d_gate_t, d_up_t = hidden.T, d_gate.T, d_up.T
        for b in range(nz):
            outs[b] += dot_nn(hidden, w_down[b])
            grad = dot_nn(hidden_t, tops[b]).astype(BF)
            for h in range(2):
                for s in range(sub):
                    start = h * half + s * part
                    dd[h, b, 0, :, s * z_depth : (s + 1) * z_depth] = grad[start : start + part]
        for b in range(nd):
            dn_ref[b] += dot_nn(d_gate, w_gu[b, 0]) + dot_nn(d_up, w_gu[b, 1])
            for which, value in ((0, d_gate_t), (1, d_up_t)):
                grad = dot_nn(value, n2_ref[b]).astype(BF)
                for h in range(2):
                    dgu[h, b, :, which, :, :depth] = grad[h * half : (h + 1) * half].reshape(sub, part, depth)
        for copy in copies(step):
            copy.start()

        @pl.when(step == nd - 1)
        def _():
            for b in range(nz):
                out_ref[:, b * z_depth : (b + 1) * z_depth] = outs[b]
            for copy in copies(step):
                copy.wait()

    def gu_spec(other):
        return pl.BlockSpec(
            (nd, sub, 1, 2 * part, depth),
            lambda i, core: (0, i, 1 - core[0] if other else core[0], 0, 0),
        )

    def down_spec(other):
        return pl.BlockSpec(
            (1, nz, 1, part, depth),
            lambda i, core: (i, 0, 1 - core[0] if other else core[0], 2, 0),
        )

    grad = shape((nd, nz, 3, part, wide), BF)
    return pl.pallas_call(
        body,
        grid_spec=pltpu.PrefetchScalarGridSpec(
            num_scalar_prefetch=1,
            grid=(nd,),
            in_specs=[
                pl.BlockSpec(blocks.shape, lambda i, core: (0, 0, 0)),
                pl.BlockSpec(top.shape, lambda i, core: (0, 0)),
                gu_spec(False),
                gu_spec(True),
                down_spec(False),
                down_spec(True),
            ],
            out_specs=(
                pl.BlockSpec((rows, width), lambda i, core: (0, 0)),
                pl.BlockSpec(blocks.shape, lambda i, core: (0, 0, 0)),
                pl.BlockSpec(memory_space=pl.ANY),
                pl.BlockSpec(memory_space=pl.ANY),
            ),
            scratch_shapes=[
                pltpu.VMEM((nz, rows, z_depth), BF),
                pltpu.VMEM((nz, rows, z_depth), F32),
                pltpu.VMEM((nd, 2, 2 * half, depth), BF),
                pltpu.VMEM((nz, 2 * half, z_depth), BF),
                pltpu.VMEM((2, nd, sub, 2, part, wide), BF),
                pltpu.VMEM((2, nz, 1, part, wide), BF),
                pltpu.SemaphoreType.DMA((4,)),
            ],
        ),
        out_shape=(shape((rows, width), F32), shape(blocks.shape, F32), grad, grad),
        compiler_params=params(),
        cost_estimate=cost(36 * rows * half * nd * width, 24 * half * nd * width, 2 * rows * half * nd),
    )(core, blocks, top, weights, weights, weights, weights)


def group_rows(ref, g):
    return jnp.concatenate(
        [ref[:, (g * GROUP + i) * HEAD_SIZE : (g * GROUP + i + 1) * HEAD_SIZE] for i in range(GROUP)],
        axis=0,
    )


def bias_of(start_ref, first_query, first_key, span, size):
    key = first_key + lax.broadcasted_iota(jnp.int32, (size, span), 0)
    query = first_query + lax.broadcasted_iota(jnp.int32, (size, span), 1)
    allowed = (key <= query) & (key >= start_ref[...])
    return jnp.concatenate([jnp.where(allowed, 0.0, masked_score)] * GROUP, axis=1)


def attend_kernel(
    span, size, pieces, info_ref, start_ref, q_ref, own, other, kv_ref, att_ref, lse_ref, acc, top, total, q_rows
):
    first_query = info_ref[0]
    for s in range(pieces):
        place = info_ref[4 + s]
        for ref, core in ((own, info_ref[3]), (other, 1 - info_ref[3])):
            kv_ref[pl.ds(pl.multiple_of((2 * place + core) * span, span), span), :] = ref[s]
    top[...] = jnp.full_like(top, lowest_top)
    total[...] = jnp.zeros_like(total)
    acc[...] = jnp.zeros_like(acc)
    value_at = KEY_VALUE_HEADS * HEAD_SIZE
    for g in range(KEY_VALUE_HEADS):
        q_rows[g] = group_rows(q_ref, g) * BF(score_scale)

    def one_block(block, carry):
        first_key = pl.multiple_of(block * size, size)
        bias = bias_of(start_ref, first_query, first_key, span, size)
        for g in range(KEY_VALUE_HEADS):
            k_at, v_at = g * HEAD_SIZE, value_at + g * HEAD_SIZE
            keys = kv_ref[pl.ds(first_key, size), k_at : k_at + HEAD_SIZE]
            values = kv_ref[pl.ds(first_key, size), v_at : v_at + HEAD_SIZE]
            scores = dot_nt(keys, q_rows[g]) + bias
            old_top = top[g]
            new_top = jnp.maximum(old_top, jnp.max(scores, axis=0, keepdims=True))
            rescale = jnp.exp(old_top - new_top)
            expo = jnp.exp(scores - new_top)
            total[g] = total[g] * rescale + jnp.sum(expo, axis=0, keepdims=True)
            acc[g] = acc[g] * rescale + dot_tn(values, expo.astype(BF))
            top[g] = new_top
        return carry

    lax.fori_loop(info_ref[1], info_ref[2], one_block, 0)
    for g in range(KEY_VALUE_HEADS):
        whole = total[g]
        result = (acc[g] * (1.0 / whole)).T.astype(BF)
        lse_ref[g] = top[g] + jnp.log(whole)
        for i in range(GROUP):
            h = g * GROUP + i
            att_ref[:, h * HEAD_SIZE : (h + 1) * HEAD_SIZE] = result[i * span : (i + 1) * span]


def attend(info, start, q, own, other, size):
    span = q.shape[0]
    rows = GROUP * span
    pieces = own.shape[0]
    length = 2 * pieces * span
    return pl.pallas_call(
        functools.partial(attend_kernel, span, size, pieces),
        out_shape=(
            jax.ShapeDtypeStruct((length, 2 * KEY_VALUE_HEADS * HEAD_SIZE), BF),
            jax.ShapeDtypeStruct((span, QUERY_HEADS * HEAD_SIZE), BF),
            jax.ShapeDtypeStruct((KEY_VALUE_HEADS, 1, rows), F32),
        ),
        in_specs=[smem_spec()] + [vmem_spec()] * 4,
        out_specs=(vmem_spec(), vmem_spec(), vmem_spec()),
        scratch_shapes=[
            pltpu.VMEM((KEY_VALUE_HEADS, HEAD_SIZE, rows), F32),
            pltpu.VMEM((KEY_VALUE_HEADS, 1, rows), F32),
            pltpu.VMEM((KEY_VALUE_HEADS, 1, rows), F32),
            pltpu.VMEM((KEY_VALUE_HEADS, rows, HEAD_SIZE), BF),
        ],
        compiler_params=params(),
        cost_estimate=cost(
            16 * QUERY_HEADS * HEAD_SIZE * span * length,
            4 * length * KEY_VALUE_HEADS * HEAD_SIZE,
            QUERY_HEADS * span * length,
        ),
    )(info, start, q, own, other)


def attend_back_kernel(
    span, size, info_ref, start_ref, q_ref, kv_ref, att_ref, datt_ref, lse_ref, cos_ref, sin_ref,
    dq_ref, dkv_ref, dq_acc, q_rows, d_rows, dot_rows,
):
    first_query = info_ref[0]
    value_at = KEY_VALUE_HEADS * HEAD_SIZE
    dq_acc[...] = jnp.zeros_like(dq_acc)
    dkv_ref[...] = jnp.zeros_like(dkv_ref)
    for g in range(KEY_VALUE_HEADS):
        grads = group_rows(datt_ref, g)
        q_rows[g] = group_rows(q_ref, g) * BF(score_scale)
        d_rows[g] = grads
        products = grads.astype(F32) * group_rows(att_ref, g).astype(F32)
        dot_rows[g] = jnp.sum(products.T, axis=0, keepdims=True)

    def one_block(block, carry):
        first_key = pl.multiple_of(block * size, size)
        bias = bias_of(start_ref, first_query, first_key, span, size)
        for g in range(KEY_VALUE_HEADS):
            k_at, v_at = g * HEAD_SIZE, value_at + g * HEAD_SIZE
            rows = q_rows[g]
            grads = d_rows[g]
            keys = kv_ref[pl.ds(first_key, size), k_at : k_at + HEAD_SIZE]
            values = kv_ref[pl.ds(first_key, size), v_at : v_at + HEAD_SIZE]
            probs = jnp.exp((dot_nt(keys, rows) + bias) - lse_ref[g])
            d_probs = dot_nt(values, grads)
            d_scores = (probs * (d_probs - dot_rows[g])).astype(BF)
            dkv_ref[pl.ds(first_key, size), v_at : v_at + HEAD_SIZE] = dot_nn(
                probs.astype(BF), grads
            ).astype(BF)
            dkv_ref[pl.ds(first_key, size), k_at : k_at + HEAD_SIZE] = dot_nn(d_scores, rows).astype(BF)
            dq_acc[g] += dot_tn(keys, d_scores)
        return carry

    lax.fori_loop(info_ref[1], info_ref[2], one_block, 0)
    cosine, sine = cos_ref[...], -sin_ref[...]
    for start in range(0, QUERY_HEADS + 1, 2):
        parts = []
        for h in (start, start + 1):
            if h < QUERY_HEADS:
                g, i = h // GROUP, h % GROUP
                parts.append(dq_acc[g, :, i * span : (i + 1) * span] * score_scale)
            else:
                parts.append(jnp.zeros((HEAD_SIZE, span), F32))
        pair = jnp.concatenate(parts, axis=0).T
        dq_ref[:, start * HEAD_SIZE : (start + 2) * HEAD_SIZE] = rotate(pair, cosine, sine).astype(BF)


def attend_back(info, start, q, kv, att, datt, lse, cosine, sine, size):
    span = q.shape[0]
    rows = GROUP * span
    length = kv.shape[0]
    per_head = (KEY_VALUE_HEADS, rows, HEAD_SIZE)
    per_row = (KEY_VALUE_HEADS, 1, rows)
    return pl.pallas_call(
        functools.partial(attend_back_kernel, span, size),
        out_shape=(
            jax.ShapeDtypeStruct((span, q.shape[1]), BF),
            jax.ShapeDtypeStruct(kv.shape, BF),
        ),
        in_specs=[smem_spec()] + [vmem_spec()] * 8,
        out_specs=(vmem_spec(), vmem_spec()),
        scratch_shapes=[
            pltpu.VMEM((KEY_VALUE_HEADS, HEAD_SIZE, rows), F32),
            pltpu.VMEM(per_head, BF),
            pltpu.VMEM(per_head, BF),
            pltpu.VMEM(per_row, F32),
        ],
        compiler_params=params(),
        cost_estimate=cost(
            40 * QUERY_HEADS * HEAD_SIZE * span * length,
            8 * length * KEY_VALUE_HEADS * HEAD_SIZE,
            QUERY_HEADS * span * length,
        ),
    )(info, start, q, kv, att, datt, lse, cosine, sine)


def in_rows(value):
    return with_layout_constraint(value, Layout(tuple(range(value.ndim))))


def after(value, *others):
    return lax.optimization_barrier((value, *others))[0]


def on_device(
    hidden_in,
    positions,
    attn_gain,
    w_query,
    key_projection_weight,
    w_value,
    w_out,
    ffn_gain,
    w_gate,
    w_up,
    w_down,
    out_grad,
):
    nd, nz = lax.axis_size("dp"), lax.axis_size("z")
    nc = 2 * nz
    seqs, span, width = hidden_in.shape
    rows = seqs * span
    length = span * nc
    d, z, c = lax.axis_index("dp"), lax.axis_index("z"), lax.axis_index("core")
    rank = 2 * z + c
    first = c == 0
    block_size = min(512, length)

    def send(value, to):
        pairs = []
        for di in range(nd):
            for zi in range(nz):
                for ci in range(2):
                    target = to(di, zi, ci)
                    if target is not None:
                        dt, zt, ct = target
                        pairs.append((di * nc + zi * 2 + ci, dt * nc + zt * 2 + ct))
        return lax.ppermute(value, ("dp", "z", "core"), pairs)

    def z_shift(value, s):
        return send(value, lambda di, zi, ci: (di, (zi + s) % nz, ci))

    def z_up(value, s):
        return send(value, lambda di, zi, ci: (di, zi + s, ci) if zi + s < nz else None)

    def z_down(value, s):
        return send(value, lambda di, zi, ci: (di, zi - s, ci) if zi >= s else None)

    def dp_xor(value, m):
        return send(value, lambda di, zi, ci: (di ^ m, zi, ci))

    def core_swap(value):
        return send(value, lambda di, zi, ci: (di, zi, 1 - ci))

    def put(buffer, piece, axis, place):
        return lax.dynamic_update_slice_in_dim(buffer, piece, place, axis)

    def take(value, axis, place):
        return lax.dynamic_index_in_dim(value, place, axis, keepdims=False)

    def in_core_order(own, other, axis):
        return jnp.stack([jnp.where(first, own, other), jnp.where(first, other, own)], axis=axis)

    dp_index = jnp.bitwise_xor(d, jnp.arange(nd, dtype=jnp.int32))
    z_index = (z - jnp.arange(nz, dtype=jnp.int32)) % nz

    def pair(left, right):
        return in_rows(jnp.stack([left.T, right.T]))

    dl = w_query.shape[0]
    own_rows = key_projection_weight.shape[1]
    early = 2 * own_rows + 8
    gain_row = jnp.concatenate([attn_gain, ffn_gain])[None]
    gain_row = jnp.pad(gain_row, ((0, 7), (0, dl - gain_row.shape[1])))
    local = [pair(key_projection_weight, w_value).reshape(-1, dl), gain_row, in_rows(w_query.T)]
    kvq_z = lax.all_gather(in_rows(jnp.concatenate(local)), "z")
    kv_own = lax.all_gather(in_rows(kvq_z[:, :early]), "dp")
    q_z = in_rows(kvq_z[:, early:])
    q_own = [q_z] + [dp_xor(after(q_z, kv_own), m) for m in range(1, nd)]
    both = in_core_order(kv_own, core_swap(kv_own), 2)
    kv_weights = both[:, :, :, : 2 * own_rows].reshape(nd, nc, 2, own_rows, dl).swapaxes(1, 2)
    kv_weights = [in_rows(take(kv_weights, 0, d ^ m).reshape(-1, dl)) for m in range(nd)]
    gains = both[0, :, :, 2 * own_rows, : 2 * (width // nc)].reshape(nc, 2, -1).swapaxes(0, 1)
    gains = gains.reshape(2, 1, width).astype(F32)
    gain_attn, gain_ffn = gains[0], gains[1]

    units = w_gate.shape[1]
    down_cut = w_down.reshape(-1, 2, units, w_down.shape[1])
    down_mine, down_away = take(down_cut, 1, c), take(down_cut, 1, 1 - c)
    down_local = in_core_order(down_mine, core_swap(down_away), 2).swapaxes(0, 1).reshape(1, units, dl)
    late_local = jnp.concatenate([pair(w_gate, w_up), down_local]).reshape(-1, dl)
    late_local = in_rows(jnp.concatenate([late_local, in_rows(w_out.T)]))
    late = lax.all_gather(late_local, ("dp", "z", "core")).reshape(nd, nz, 2, -1, dl)

    lane = np.arange(128)
    frequency = jnp.power(theta_base, -jnp.asarray(lane % HALF, F32) * 2.0 / HEAD_SIZE)
    angle = positions.reshape(rows, 1).astype(F32) * frequency[None, :]
    cosine = jnp.cos(angle)
    sine = jnp.sin(angle) * jnp.asarray(np.where(lane % HEAD_SIZE < HALF, -1.0, 1.0), F32)[None, :]

    hidden_rows = hidden_in.reshape(rows, width)
    top_grad = out_grad.reshape(rows, width)
    one_blocks, kv_here = keys_values(hidden_rows, gain_attn, dp_index, kv_weights, cosine, sine)

    first_query = rank * span
    kv_up = []
    for i in range(seqs):
        piece = kv_here[i * span : (i + 1) * span]
        if i:
            piece = after(piece, kv_up[-1][1])
        kv_up.append([piece] + [z_up(piece, s) for s in range(1, nz)])

    q_own = jnp.stack([after(piece, kv_here) for piece in q_own])
    q_weights = in_core_order(q_own, core_swap(q_own), 2).reshape(nd, -1, dl)
    padding = -(QUERY_HEADS * HEAD_SIZE) % 128
    q_weights = [in_rows(jnp.pad(q_weights[m], ((0, padding), (0, 0)))) for m in range(nd)]
    one_blocks = after(one_blocks, kv_up[0][1])
    query = queries(one_blocks, dp_index, q_weights, cosine, sine)
    att_list, lse_list, kv_list, info_list, start_list = [], [], [], [], []
    for i in range(seqs):
        begin = (first_query + jnp.arange(span, dtype=jnp.int32) - positions[i]).reshape(1, span)
        info = jnp.concatenate(
            [
                jnp.stack(
                    [first_query, begin[0, 0] // block_size, (first_query + span - 1) // block_size + 1, c]
                ),
                z_index,
            ]
        ).astype(jnp.int32)
        own = [after(piece, att_list[-1]) for piece in kv_up[i]] if i else kv_up[i]
        own = jnp.stack(own)
        kv, att, lse = attend(info, begin, query[i * span : (i + 1) * span], own, core_swap(own), block_size)
        att_list.append(att)
        lse_list.append(lse)
        kv_list.append(kv)
        info_list.append(info)
        start_list.append(begin)
    late = after(late, att_list[0])
    o_weights = late[:, :, :, 3 * units :].reshape(nd, width, dl)
    o_weights = [in_rows(take(o_weights, 0, d ^ m)) for m in range(nd)]
    att_blocks, mid, two_blocks = middle(att_list, hidden_rows, gain_ffn, dp_index, o_weights)

    made, dn, ffn_grad, ffn_away = feed_forward(
        c.reshape(1).astype(jnp.int32), two_blocks, top_grad, late, units
    )
    layer_out, grad_mid, grad_att, do, ffn_sum = middle_back(
        mid, top_grad, gain_ffn, dp_index, att_blocks, made, dn, o_weights
    )

    def add(*values):
        total = values[0].astype(F32)
        for value in values[1:]:
            total = total + value.astype(F32)
        return total

    def over_dp(value):
        return add(value[0], *[dp_xor(value[m], m) for m in range(1, nd)])

    def z_pieces(value):
        return [take(value, 0, z)] + [z_shift(take(value, 0, (z + s) % nz), s) for s in range(1, nz)]

    def over_z(value):
        return add(*z_pieces(value))

    def rows_of(value, parts):
        cut = value.reshape(nd, parts, nz, 2, -1, value.shape[-1])

        def half(which):
            return take(cut, 3, which).transpose(0, 2, 1, 3, 4).reshape(nd, nz, -1, value.shape[-1])

        return half(c), half(1 - c)

    def finish(value):
        return in_rows(over_z(value.reshape(nz, -1, value.shape[-1]))).T

    ffn_grad = add(ffn_grad, after(core_swap(ffn_away), grad_att)).astype(BF)
    grad_att = after(grad_att, ffn_grad)
    ffn_grad = in_rows(ffn_grad.reshape(nd, -1, ffn_grad.shape[-1]))
    ffn_scattered = in_rows(lax.psum_scatter(ffn_grad, "dp", scatter_dimension=0, tiled=True))
    dq_list, dkv_list = [], []
    for i in range(seqs):
        here = slice(i * span, (i + 1) * span)
        grad_here = grad_att[here]
        if i:
            grad_here = after(grad_here, mine)
        dq, dkv = attend_back(
            info_list[i], start_list[i], query[here], kv_list[i], att_list[i], grad_here, lse_list[i],
            cosine[here], sine[here], block_size,
        )
        if i:
            dkv = after(dkv, *dkv_list[-1])
        cut = dkv.reshape(nz, 2, span, dkv.shape[-1])
        mine = add(take(cut, 1, c), core_swap(take(cut, 1, 1 - c))).astype(BF)
        dkv_list.append(
            [take(mine, 0, z)] + [z_down(take(mine, 0, (z - s) % nz), s) for s in range(1, nz)]
        )
        dq_list.append(dq)
    dx_blocks, dq_w = queries_back([after(dq, mine) for dq in dq_list], one_blocks, dp_index, q_weights)
    do_mine, do_other = rows_of(do, 1)
    q_mine, q_other = rows_of(dq_w[:, : QUERY_HEADS * HEAD_SIZE], 1)
    dqo = core_swap(after(jnp.concatenate([q_other, do_other], axis=2), *dkv_list[-1]))
    dqo = add(jnp.concatenate([q_mine, do_mine], axis=2), dqo).astype(BF)
    dx_blocks = after(dx_blocks, ffn_scattered)
    ffn_pieces = z_pieces(ffn_scattered.reshape(nz, 3, units, -1))
    dqo = finish(after(over_dp(dqo).astype(BF), ffn_pieces[2]))
    w_query_grad, w_out_grad = jnp.split(dqo, 2, axis=1)

    input_grad, dkv_w, attn_sum = keys_values_back(
        dkv_list, one_blocks, dx_blocks, grad_mid, hidden_rows, gain_attn, dp_index, kv_weights, cosine, sine
    )
    dkv_w = after(dkv_w, ffn_pieces[1], ffn_pieces[-1])
    kv_mine, kv_other = rows_of(dkv_w, 2)
    sums = jnp.concatenate([attn_sum, ffn_sum]).reshape(2, nz, 2, -1).transpose(2, 1, 0, 3).reshape(2, nz, 1, -1)
    sums = jnp.pad(sums, ((0, 0), (0, 0), (0, 7), (0, dl - sums.shape[3]))).astype(BF)

    def with_sums(value, which):
        more = jnp.broadcast_to(take(sums, 0, which)[None], (nd,) + sums.shape[1:])
        return jnp.concatenate([value, more], axis=2)

    dkv_from = core_swap(with_sums(kv_other, 1 - c))
    dkv_w = add(with_sums(kv_mine, c), dkv_from).astype(BF)
    dkv_w = in_rows(over_z(over_dp(dkv_w).astype(BF)))
    w_key_grad, w_value_grad = dkv_w[:own_rows].T, dkv_w[own_rows : 2 * own_rows].T
    gain_own = dkv_w[2 * own_rows, : 2 * (width // nc)].reshape(2, -1)
    ffn_grad = in_rows(add(*ffn_pieces)[:, :, :dl])
    w_gate_grad, w_up_grad = ffn_grad[0].T, ffn_grad[1].T
    down_cut = ffn_grad[2].reshape(units, -1, 2, w_down.shape[1]).swapaxes(0, 1)
    down_from = core_swap(take(down_cut, 2, 1 - c))
    w_down_grad = in_core_order(take(down_cut, 2, c), down_from, 1).reshape(w_down.shape)

    return (
        layer_out.reshape(seqs, span, width),
        input_grad.reshape(seqs, span, width),
        gain_own[0],
        w_query_grad,
        w_key_grad,
        w_value_grad,
        w_out_grad,
        gain_own[1],
        w_gate_grad,
        w_up_grad,
        w_down_grad,
    )


def solution(mesh):
    mesh = jax.sharding.Mesh(
        mesh.devices.reshape(mesh.shape["dp"], mesh.shape["ctx"] // 2, 2), ("dp", "z", "core")
    )
    placed = (
        P("dp", ("z", "core"), None),
        P("dp", ("z", "core")),
        P(("z", "core")),
        P("dp", ("z", "core")),
        P("dp", ("z", "core")),
        P("dp", ("z", "core")),
        P("dp", ("z", "core")),
        P(("z", "core")),
        P("dp", ("z", "core")),
        P("dp", ("z", "core")),
        P("dp", ("z", "core")),
        P("dp", ("z", "core"), None),
    )
    return jax.shard_map(
        on_device,
        mesh=mesh,
        in_specs=placed,
        out_specs=(
            P("dp", ("z", "core"), None),
            P("dp", ("z", "core"), None),
            P(("z", "core")),
            P("dp", ("z", "core")),
            P("dp", ("z", "core")),
            P("dp", ("z", "core")),
            P("dp", ("z", "core")),
            P(("z", "core")),
            P("dp", ("z", "core")),
            P("dp", ("z", "core")),
            P("dp", ("z", "core")),
        ),
        check_vma=False,
    )
```

```python
import functools

import jax
import jax.numpy as jnp
import numpy as np
from jax import lax
from jax.experimental import pallas as pl
from jax.experimental.layout import Layout, with_layout_constraint
from jax.experimental.pallas import tpu as pltpu
from jax.sharding import PartitionSpec as P

QUERY_HEADS = 15
KEY_VALUE_HEADS = 5
HEAD_SIZE = 64
GROUP = QUERY_HEADS // KEY_VALUE_HEADS
HALF = HEAD_SIZE // 2

epsilon = 1e-05
theta_base = 100000.0
masked_score = -1e30
lowest_top = -1e29
score_scale = 0.125
VMEM_BYTES = 56 * 1024 * 1024

BF = jnp.bfloat16
F32 = jnp.float32


def dot_nn(a, b):
    return lax.dot_general(a, b, (((1,), (0,)), ((), ())), preferred_element_type=F32)


def dot_nt(a, b):
    return lax.dot_general(a, b, (((1,), (1,)), ((), ())), preferred_element_type=F32)


def dot_tn(a, b):
    return lax.dot_general(a, b, (((0,), (0,)), ((), ())), preferred_element_type=F32)


def vmem_spec():
    return pl.BlockSpec(memory_space=pltpu.VMEM)


def smem_spec():
    return pl.BlockSpec(memory_space=pltpu.SMEM)


def params():
    return pltpu.CompilerParams(vmem_limit_bytes=VMEM_BYTES)


def cost(flops, bytes_accessed, transcendentals=0):
    part = 64
    return pl.CostEstimate(
        flops=int(flops) // part,
        bytes_accessed=int(bytes_accessed) // part,
        transcendentals=int(transcendentals) // part,
    )


def rotate(value, cosine, sine, limit=None):
    width = value.shape[1]
    lane = lax.broadcasted_iota(jnp.int32, value.shape, 1)
    ahead = pltpu.roll(value, width - HALF, 1)
    behind = pltpu.roll(value, HALF, 1)
    swapped = jnp.where(lane % HEAD_SIZE < HALF, ahead, behind)
    copies = width // 128
    cos_wide = jnp.concatenate([cosine] * copies, axis=1)
    sin_wide = jnp.concatenate([sine] * copies, axis=1)
    turned = value * cos_wide + swapped * sin_wide
    if limit is not None:
        turned = jnp.where(lane < limit, turned, value)
    return turned


def row_chunks(rows):
    size = min(128, rows)
    return [slice(start, start + size) for start in range(0, rows, size)]


def column_chunks(columns):
    return [slice(start, min(start + 256, columns)) for start in range(0, columns, 256)]


def scale_of(value):
    return lax.rsqrt(jnp.mean(value * value, axis=1, keepdims=True) + epsilon)


def call(body, operands, n_smem, outs, flops, scratch=()):
    moved = sum(o.size * o.dtype.itemsize for o in operands) + sum(
        int(np.prod(o.shape)) * o.dtype.itemsize for o in outs
    )
    return pl.pallas_call(
        body,
        out_shape=tuple(outs),
        in_specs=[smem_spec()] * n_smem + [vmem_spec()] * (len(operands) - n_smem),
        out_specs=tuple(vmem_spec() for _ in outs),
        scratch_shapes=list(scratch),
        compiler_params=params(),
        cost_estimate=cost(flops, moved),
    )(*operands)


def shape(dims, dtype):
    return jax.ShapeDtypeStruct(tuple(dims), dtype)


def block_product(x_ref, index_ref, weights, columns):
    total = None
    for m, weight in enumerate(weights):
        term = dot_nt(x_ref[index_ref[m]], weight[columns, :])
        total = term if total is None else total + term
    return total


def keys_values(hidden, gain, index, weights, cosine, sine):
    nd = len(weights)
    rows, width = hidden.shape
    depth = width // nd
    columns = weights[0].shape[0]
    turn = KEY_VALUE_HEADS * HEAD_SIZE

    def body(index_ref, hidden_ref, gain_ref, cos_ref, sin_ref, *rest):
        w, (blocks_ref, kv_ref) = rest[:nd], rest[nd:]
        for here in row_chunks(rows):
            x = hidden_ref[here, :].astype(F32)
            normed = (x * scale_of(x) * gain_ref[...]).astype(BF)
            for b in range(nd):
                blocks_ref[b, here, :] = normed[:, b * depth : (b + 1) * depth]
        for cols in column_chunks(columns):
            total = block_product(blocks_ref, index_ref, w, cols)
            if turn > cols.start:
                total = rotate(total, cos_ref[...], sin_ref[...], turn - cols.start if turn < cols.stop else None)
            kv_ref[:, cols] = total.astype(BF)

    return call(
        body,
        [index, hidden, gain, cosine, sine, *weights],
        1,
        [shape((nd, rows, depth), BF), shape((rows, columns), BF)],
        2 * rows * columns * width,
    )


def queries(blocks, index, weights, cosine, sine):
    nd, rows, depth = blocks.shape
    columns = weights[0].shape[0]

    def body(index_ref, blocks_ref, cos_ref, sin_ref, *rest):
        w, out_ref = rest[:nd], rest[nd]
        for cols in column_chunks(columns):
            total = block_product(blocks_ref, index_ref, w, cols)
            out_ref[:, cols] = rotate(total, cos_ref[...], sin_ref[...]).astype(BF)

    return call(
        body,
        [index, blocks, cosine, sine, *weights],
        1,
        [shape((rows, columns), BF)],
        2 * rows * columns * nd * depth,
    )[0]


def middle(att_parts, hidden, gain, index, weights):
    nd = len(weights)
    parts = len(att_parts)
    rows, width = hidden.shape
    depth = width // nd
    span = rows // parts

    def body(index_ref, hidden_ref, gain_ref, *rest):
        att, w = rest[:parts], rest[parts : parts + nd]
        att_ref, mid_ref, two_ref = rest[parts + nd :]
        for p in range(parts):
            for b in range(nd):
                att_ref[b, p * span : (p + 1) * span, :] = att[p][:, b * depth : (b + 1) * depth]
        for cols in column_chunks(width):
            mid_ref[:, cols] = hidden_ref[:, cols].astype(F32) + block_product(att_ref, index_ref, w, cols)
        for here in row_chunks(rows):
            x = mid_ref[here, :]
            normed = (x * scale_of(x) * gain_ref[...]).astype(BF)
            for b in range(nd):
                two_ref[b, here, :] = normed[:, b * depth : (b + 1) * depth]

    return call(
        body,
        [index, hidden, gain, *att_parts, *weights],
        1,
        [
            shape((nd, rows, depth), BF),
            shape((rows, width), F32),
            shape((nd, rows, depth), BF),
        ],
        2 * rows * width * width,
    )


def middle_back(mid, out_grad, gain, index, att_blocks, made, dn, weights):
    nd = len(weights)
    rows, width = mid.shape
    depth = width // nd

    def body(index_ref, mid_ref, grad_ref, gain_ref, att_ref, made_ref, dn_ref, *rest):
        w = rest[:nd]
        layer_ref, dmid_ref, datt_ref, dw_ref, sum_ref, low_ref, block_ref = rest[nd:]
        sums = jnp.zeros((1, width), F32)
        for here in row_chunks(rows):
            x = mid_ref[here, :]
            up = grad_ref[here, :].astype(F32)
            layer_ref[here, :] = (x + made_ref[here, :]).astype(BF)
            dn = jnp.concatenate([dn_ref[b, here, :] for b in range(nd)], axis=1)
            scale = scale_of(x)
            weighted = dn * gain_ref[...]
            sums += jnp.sum(dn * x * scale, axis=0, keepdims=True)
            inner = jnp.mean(weighted * x, axis=1, keepdims=True)
            dmid = up + scale * weighted - x * (scale * scale * scale * inner)
            dmid_ref[here, :] = dmid
            low_ref[here, :] = dmid.astype(BF)
        sum_ref[...] = sums
        for m in range(nd):
            block_ref[index_ref[m]] = dot_nn(low_ref[...], w[m][...])
        for cols in column_chunks(width):
            turned = low_ref[:, cols].T
            for m in range(nd):
                dw_ref[m, cols, :] = dot_nn(turned, att_ref[index_ref[m]]).astype(BF)
        for b in range(nd):
            datt_ref[:, b * depth : (b + 1) * depth] = block_ref[b].astype(BF)

    return call(
        body,
        [index, mid, out_grad, gain, att_blocks, made, dn, *weights],
        1,
        [
            shape((rows, width), BF),
            shape((rows, width), F32),
            shape((rows, width), BF),
            shape((nd, width, depth), BF),
            shape((1, width), F32),
        ],
        4 * rows * width * width,
        [pltpu.VMEM((rows, width), BF), pltpu.VMEM((nd, rows, depth), F32)],
    )


def queries_back(dq_parts, blocks, index, weights):
    nd, rows, depth = blocks.shape
    parts = len(dq_parts)
    span = rows // parts
    columns = weights[0].shape[0]

    def body(index_ref, blocks_ref, *rest):
        dq, w = rest[:parts], rest[parts : parts + nd]
        dx_ref, dw_ref, all_ref = rest[parts + nd :]
        for p in range(parts):
            all_ref[p * span : (p + 1) * span, :] = dq[p][...]
        for m in range(nd):
            dx_ref[index_ref[m]] = dot_nn(all_ref[...], w[m][...])
        for cols in column_chunks(columns):
            turned = all_ref[:, cols].T
            for m in range(nd):
                dw_ref[m, cols, :] = dot_nn(turned, blocks_ref[index_ref[m]]).astype(BF)

    return call(
        body,
        [index, blocks, *dq_parts, *weights],
        1,
        [shape((nd, rows, depth), F32), shape((nd, columns, depth), BF)],
        4 * rows * columns * nd * depth,
        [pltpu.VMEM((rows, columns), BF)],
    )


def keys_values_back(dkv_parts, blocks, dx_blocks, dmid, hidden, gain, index, weights, cosine, sine):
    nd, rows, depth = blocks.shape
    parts = len(dkv_parts)
    columns = weights[0].shape[0]
    width = nd * depth
    turn = KEY_VALUE_HEADS * HEAD_SIZE
    pieces = len(dkv_parts[0])
    flat = [piece for part in dkv_parts for piece in part]
    span = rows // parts

    def body(index_ref, blocks_ref, dx_ref, dmid_ref, hidden_ref, gain_ref, cos_ref, sin_ref, *rest):
        got, w = rest[: parts * pieces], rest[parts * pieces : parts * pieces + nd]
        grad_ref, dw_ref, sum_ref, low_ref, block_ref = rest[parts * pieces + nd :]
        for p in range(parts):
            here = slice(p * span, (p + 1) * span)
            for cols in column_chunks(columns):
                total = got[p * pieces][:, cols].astype(F32)
                for piece in got[p * pieces + 1 : (p + 1) * pieces]:
                    total = total + piece[:, cols].astype(F32)
                if turn > cols.start:
                    limit = turn - cols.start if turn < cols.stop else None
                    total = rotate(total, cos_ref[here, :], -sin_ref[here, :], limit)
                low_ref[here, cols] = total.astype(BF)
        for m in range(nd):
            place = index_ref[m]
            block_ref[place] = dx_ref[place] + dot_nn(low_ref[...], w[m][...])
        for cols in column_chunks(columns):
            turned = low_ref[:, cols].T
            for m in range(nd):
                dw_ref[m, cols, :] = dot_nn(turned, blocks_ref[index_ref[m]]).astype(BF)
        sums = jnp.zeros((1, width), F32)
        for here in row_chunks(rows):
            x = hidden_ref[here, :].astype(F32)
            dn = jnp.concatenate([block_ref[b, here, :] for b in range(nd)], axis=1)
            scale = scale_of(x)
            weighted = dn * gain_ref[...]
            sums += jnp.sum(dn * x * scale, axis=0, keepdims=True)
            inner = jnp.mean(weighted * x, axis=1, keepdims=True)
            grad = dmid_ref[here, :] + scale * weighted - x * (scale * scale * scale * inner)
            grad_ref[here, :] = grad.astype(BF)
        sum_ref[...] = sums

    return call(
        body,
        [index, blocks, dx_blocks, dmid, hidden, gain, cosine, sine, *flat, *weights],
        1,
        [shape((rows, width), BF), shape((nd, columns, depth), BF), shape((1, width), F32)],
        4 * rows * columns * width,
        [pltpu.VMEM((rows, columns), BF), pltpu.VMEM((nd, rows, depth), F32)],
    )


def feed_forward(core, blocks, top, weights, part):
    nd, nz, _, _, depth = weights.shape
    wide = depth + -depth % 128
    rows, width = top.shape
    sub = nz // nd
    half = sub * part
    z_depth = width // nz

    def body(
        core_ref, n2_ref, top_ref, gu_own, gu_other, down_own, down_other, out_ref, dn_ref, dw_own, dw_other,
        tops, outs, w_gu, w_down, dgu, dd, sems,
    ):
        step = pl.program_id(0)

        def copies(at):
            made = []
            for h, ref in enumerate((dw_own, dw_other)):
                made.append(
                    pltpu.make_async_copy(
                        dgu.at[h], ref.at[:, pl.ds(at * sub, sub), pl.ds(0, 2)], sems.at[2 * h]
                    )
                )
                made.append(
                    pltpu.make_async_copy(dd.at[h], ref.at[at, :, pl.ds(2, 1)], sems.at[2 * h + 1])
                )
            return made

        @pl.when(step == 0)
        def _():
            dn_ref[...] = jnp.zeros_like(dn_ref)
            outs[...] = jnp.zeros_like(outs)
            dgu[...] = jnp.zeros_like(dgu)
            dd[...] = jnp.zeros_like(dd)
            for b in range(nz):
                tops[b] = top_ref[:, b * z_depth : (b + 1) * z_depth]

        for h, (gu, down) in enumerate(((gu_own, down_own), (gu_other, down_other))):
            here = slice(h * half, (h + 1) * half)
            for b in range(nd):
                for which in range(2):
                    w_gu[b, which, here, :] = gu[b, :, 0, which * part : (which + 1) * part].reshape(half, depth)
            for b in range(nz):
                for s in range(sub):
                    w_down[b, h * half + s * part : h * half + (s + 1) * part, :] = down[
                        0, b, 0, :, s * z_depth : (s + 1) * z_depth
                    ]

        gate = up = grad_hidden = None
        for b in range(nd):
            term_g = dot_nt(n2_ref[b], w_gu[b, 0])
            term_u = dot_nt(n2_ref[b], w_gu[b, 1])
            gate = term_g if gate is None else gate + term_g
            up = term_u if up is None else up + term_u
        for b in range(nz):
            term = dot_nt(tops[b], w_down[b])
            grad_hidden = term if grad_hidden is None else grad_hidden + term
        sig = jax.nn.sigmoid(gate)
        act = gate * sig
        hidden = (act * up).astype(BF)
        d_gate = (grad_hidden * up * sig * (1.0 + gate * (1.0 - sig))).astype(BF)
        d_up = (grad_hidden * act).astype(BF)

        @pl.when(step > 0)
        def _():
            for copy in copies(step - 1):
                copy.wait()

        hidden_t, d_gate_t, d_up_t = hidden.T, d_gate.T, d_up.T
        for b in range(nz):
            outs[b] += dot_nn(hidden, w_down[b])
            grad = dot_nn(hidden_t, tops[b]).astype(BF)
            for h in range(2):
                for s in range(sub):
                    start = h * half + s * part
                    dd[h, b, 0, :, s * z_depth : (s + 1) * z_depth] = grad[start : start + part]
        for b in range(nd):
            dn_ref[b] += dot_nn(d_gate, w_gu[b, 0]) + dot_nn(d_up, w_gu[b, 1])
            for which, value in ((0, d_gate_t), (1, d_up_t)):
                grad = dot_nn(value, n2_ref[b]).astype(BF)
                for h in range(2):
                    dgu[h, b, :, which, :, :depth] = grad[h * half : (h + 1) * half].reshape(sub, part, depth)
        for copy in copies(step):
            copy.start()

        @pl.when(step == nd - 1)
        def _():
            for b in range(nz):
                out_ref[:, b * z_depth : (b + 1) * z_depth] = outs[b]
            for copy in copies(step):
                copy.wait()

    def gu_spec(other):
        return pl.BlockSpec(
            (nd, sub, 1, 2 * part, depth),
            lambda i, core: (0, i, 1 - core[0] if other else core[0], 0, 0),
        )

    def down_spec(other):
        return pl.BlockSpec(
            (1, nz, 1, part, depth),
            lambda i, core: (i, 0, 1 - core[0] if other else core[0], 2, 0),
        )

    grad = shape((nd, nz, 3, part, wide), BF)
    return pl.pallas_call(
        body,
        grid_spec=pltpu.PrefetchScalarGridSpec(
            num_scalar_prefetch=1,
            grid=(nd,),
            in_specs=[
                pl.BlockSpec(blocks.shape, lambda i, core: (0, 0, 0)),
                pl.BlockSpec(top.shape, lambda i, core: (0, 0)),
                gu_spec(False),
                gu_spec(True),
                down_spec(False),
                down_spec(True),
            ],
            out_specs=(
                pl.BlockSpec((rows, width), lambda i, core: (0, 0)),
                pl.BlockSpec(blocks.shape, lambda i, core: (0, 0, 0)),
                pl.BlockSpec(memory_space=pl.ANY),
                pl.BlockSpec(memory_space=pl.ANY),
            ),
            scratch_shapes=[
                pltpu.VMEM((nz, rows, z_depth), BF),
                pltpu.VMEM((nz, rows, z_depth), F32),
                pltpu.VMEM((nd, 2, 2 * half, depth), BF),
                pltpu.VMEM((nz, 2 * half, z_depth), BF),
                pltpu.VMEM((2, nd, sub, 2, part, wide), BF),
                pltpu.VMEM((2, nz, 1, part, wide), BF),
                pltpu.SemaphoreType.DMA((4,)),
            ],
        ),
        out_shape=(shape((rows, width), F32), shape(blocks.shape, F32), grad, grad),
        compiler_params=params(),
        cost_estimate=cost(36 * rows * half * nd * width, 24 * half * nd * width, 2 * rows * half * nd),
    )(core, blocks, top, weights, weights, weights, weights)


def group_rows(ref, g):
    return jnp.concatenate(
        [ref[:, (g * GROUP + i) * HEAD_SIZE : (g * GROUP + i + 1) * HEAD_SIZE] for i in range(GROUP)],
        axis=0,
    )


def bias_of(start_ref, first_query, first_key, span, size):
    key = first_key + lax.broadcasted_iota(jnp.int32, (size, span), 0)
    query = first_query + lax.broadcasted_iota(jnp.int32, (size, span), 1)
    allowed = (key <= query) & (key >= start_ref[...])
    return jnp.concatenate([jnp.where(allowed, 0.0, masked_score)] * GROUP, axis=1)


def attend_kernel(
    span, size, pieces, info_ref, start_ref, q_ref, own, other, kv_ref, att_ref, lse_ref, acc, top, total, q_rows
):
    first_query = info_ref[0]
    for s in range(pieces):
        place = info_ref[4 + s]
        for ref, core in ((own, info_ref[3]), (other, 1 - info_ref[3])):
            kv_ref[pl.ds(pl.multiple_of((2 * place + core) * span, span), span), :] = ref[s]
    top[...] = jnp.full_like(top, lowest_top)
    total[...] = jnp.zeros_like(total)
    acc[...] = jnp.zeros_like(acc)
    value_at = KEY_VALUE_HEADS * HEAD_SIZE
    for g in range(KEY_VALUE_HEADS):
        q_rows[g] = group_rows(q_ref, g) * BF(score_scale)

    def one_block(block, carry):
        first_key = pl.multiple_of(block * size, size)
        bias = bias_of(start_ref, first_query, first_key, span, size)
        for g in range(KEY_VALUE_HEADS):
            k_at, v_at = g * HEAD_SIZE, value_at + g * HEAD_SIZE
            keys = kv_ref[pl.ds(first_key, size), k_at : k_at + HEAD_SIZE]
            values = kv_ref[pl.ds(first_key, size), v_at : v_at + HEAD_SIZE]
            scores = dot_nt(keys, q_rows[g]) + bias
            old_top = top[g]
            new_top = jnp.maximum(old_top, jnp.max(scores, axis=0, keepdims=True))
            rescale = jnp.exp(old_top - new_top)
            expo = jnp.exp(scores - new_top)
            total[g] = total[g] * rescale + jnp.sum(expo, axis=0, keepdims=True)
            acc[g] = acc[g] * rescale + dot_tn(values, expo.astype(BF))
            top[g] = new_top
        return carry

    lax.fori_loop(info_ref[1], info_ref[2], one_block, 0)
    for g in range(KEY_VALUE_HEADS):
        whole = total[g]
        result = (acc[g] * (1.0 / whole)).T.astype(BF)
        lse_ref[g] = top[g] + jnp.log(whole)
        for i in range(GROUP):
            h = g * GROUP + i
            att_ref[:, h * HEAD_SIZE : (h + 1) * HEAD_SIZE] = result[i * span : (i + 1) * span]


def attend(info, start, q, own, other, size):
    span = q.shape[0]
    rows = GROUP * span
    pieces = own.shape[0]
    length = 2 * pieces * span
    return pl.pallas_call(
        functools.partial(attend_kernel, span, size, pieces),
        out_shape=(
            jax.ShapeDtypeStruct((length, 2 * KEY_VALUE_HEADS * HEAD_SIZE), BF),
            jax.ShapeDtypeStruct((span, QUERY_HEADS * HEAD_SIZE), BF),
            jax.ShapeDtypeStruct((KEY_VALUE_HEADS, 1, rows), F32),
        ),
        in_specs=[smem_spec()] + [vmem_spec()] * 4,
        out_specs=(vmem_spec(), vmem_spec(), vmem_spec()),
        scratch_shapes=[
            pltpu.VMEM((KEY_VALUE_HEADS, HEAD_SIZE, rows), F32),
            pltpu.VMEM((KEY_VALUE_HEADS, 1, rows), F32),
            pltpu.VMEM((KEY_VALUE_HEADS, 1, rows), F32),
            pltpu.VMEM((KEY_VALUE_HEADS, rows, HEAD_SIZE), BF),
        ],
        compiler_params=params(),
        cost_estimate=cost(
            16 * QUERY_HEADS * HEAD_SIZE * span * length,
            4 * length * KEY_VALUE_HEADS * HEAD_SIZE,
            QUERY_HEADS * span * length,
        ),
    )(info, start, q, own, other)


def attend_back_kernel(
    span, size, info_ref, start_ref, q_ref, kv_ref, att_ref, datt_ref, lse_ref, cos_ref, sin_ref,
    dq_ref, dkv_ref, dq_acc, q_rows, d_rows, dot_rows,
):
    first_query = info_ref[0]
    value_at = KEY_VALUE_HEADS * HEAD_SIZE
    dq_acc[...] = jnp.zeros_like(dq_acc)
    dkv_ref[...] = jnp.zeros_like(dkv_ref)
    for g in range(KEY_VALUE_HEADS):
        grads = group_rows(datt_ref, g)
        q_rows[g] = group_rows(q_ref, g) * BF(score_scale)
        d_rows[g] = grads
        products = grads.astype(F32) * group_rows(att_ref, g).astype(F32)
        dot_rows[g] = jnp.sum(products.T, axis=0, keepdims=True)

    def one_block(block, carry):
        first_key = pl.multiple_of(block * size, size)
        bias = bias_of(start_ref, first_query, first_key, span, size)
        for g in range(KEY_VALUE_HEADS):
            k_at, v_at = g * HEAD_SIZE, value_at + g * HEAD_SIZE
            rows = q_rows[g]
            grads = d_rows[g]
            keys = kv_ref[pl.ds(first_key, size), k_at : k_at + HEAD_SIZE]
            values = kv_ref[pl.ds(first_key, size), v_at : v_at + HEAD_SIZE]
            probs = jnp.exp((dot_nt(keys, rows) + bias) - lse_ref[g])
            d_probs = dot_nt(values, grads)
            d_scores = (probs * (d_probs - dot_rows[g])).astype(BF)
            dkv_ref[pl.ds(first_key, size), v_at : v_at + HEAD_SIZE] = dot_nn(
                probs.astype(BF), grads
            ).astype(BF)
            dkv_ref[pl.ds(first_key, size), k_at : k_at + HEAD_SIZE] = dot_nn(d_scores, rows).astype(BF)
            dq_acc[g] += dot_tn(keys, d_scores)
        return carry

    lax.fori_loop(info_ref[1], info_ref[2], one_block, 0)
    cosine, sine = cos_ref[...], -sin_ref[...]
    for start in range(0, QUERY_HEADS + 1, 2):
        parts = []
        for h in (start, start + 1):
            if h < QUERY_HEADS:
                g, i = h // GROUP, h % GROUP
                parts.append(dq_acc[g, :, i * span : (i + 1) * span] * score_scale)
            else:
                parts.append(jnp.zeros((HEAD_SIZE, span), F32))
        pair = jnp.concatenate(parts, axis=0).T
        dq_ref[:, start * HEAD_SIZE : (start + 2) * HEAD_SIZE] = rotate(pair, cosine, sine).astype(BF)


def attend_back(info, start, q, kv, att, datt, lse, cosine, sine, size):
    span = q.shape[0]
    rows = GROUP * span
    length = kv.shape[0]
    per_head = (KEY_VALUE_HEADS, rows, HEAD_SIZE)
    per_row = (KEY_VALUE_HEADS, 1, rows)
    return pl.pallas_call(
        functools.partial(attend_back_kernel, span, size),
        out_shape=(
            jax.ShapeDtypeStruct((span, q.shape[1]), BF),
            jax.ShapeDtypeStruct(kv.shape, BF),
        ),
        in_specs=[smem_spec()] + [vmem_spec()] * 8,
        out_specs=(vmem_spec(), vmem_spec()),
        scratch_shapes=[
            pltpu.VMEM((KEY_VALUE_HEADS, HEAD_SIZE, rows), F32),
            pltpu.VMEM(per_head, BF),
            pltpu.VMEM(per_head, BF),
            pltpu.VMEM(per_row, F32),
        ],
        compiler_params=params(),
        cost_estimate=cost(
            40 * QUERY_HEADS * HEAD_SIZE * span * length,
            8 * length * KEY_VALUE_HEADS * HEAD_SIZE,
            QUERY_HEADS * span * length,
        ),
    )(info, start, q, kv, att, datt, lse, cosine, sine)


def in_rows(value):
    return with_layout_constraint(value, Layout(tuple(range(value.ndim))))


def after(value, *others):
    return lax.optimization_barrier((value, *others))[0]


def on_device(
    hidden_in,
    positions,
    attn_gain,
    w_query,
    key_projection_weight,
    w_value,
    w_out,
    ffn_gain,
    w_gate,
    w_up,
    w_down,
    out_grad,
):
    nd, nz = lax.axis_size("dp"), lax.axis_size("z")
    nc = 2 * nz
    seqs, span, width = hidden_in.shape
    rows = seqs * span
    length = span * nc
    d, z, c = lax.axis_index("dp"), lax.axis_index("z"), lax.axis_index("core")
    rank = 2 * z + c
    first = c == 0
    block_size = min(512, length)

    def send(value, to):
        pairs = []
        for di in range(nd):
            for zi in range(nz):
                for ci in range(2):
                    target = to(di, zi, ci)
                    if target is not None:
                        dt, zt, ct = target
                        pairs.append((di * nc + zi * 2 + ci, dt * nc + zt * 2 + ct))
        return lax.ppermute(value, ("dp", "z", "core"), pairs)

    def z_shift(value, s):
        return send(value, lambda di, zi, ci: (di, (zi + s) % nz, ci))

    def z_up(value, s):
        return send(value, lambda di, zi, ci: (di, zi + s, ci) if zi + s < nz else None)

    def z_down(value, s):
        return send(value, lambda di, zi, ci: (di, zi - s, ci) if zi >= s else None)

    def dp_xor(value, m):
        return send(value, lambda di, zi, ci: (di ^ m, zi, ci))

    def core_swap(value):
        return send(value, lambda di, zi, ci: (di, zi, 1 - ci))

    def put(buffer, piece, axis, place):
        return lax.dynamic_update_slice_in_dim(buffer, piece, place, axis)

    def take(value, axis, place):
        return lax.dynamic_index_in_dim(value, place, axis, keepdims=False)

    def in_core_order(own, other, axis):
        return jnp.stack([jnp.where(first, own, other), jnp.where(first, other, own)], axis=axis)

    dp_index = jnp.bitwise_xor(d, jnp.arange(nd, dtype=jnp.int32))
    z_index = (z - jnp.arange(nz, dtype=jnp.int32)) % nz

    def pair(left, right):
        return in_rows(jnp.stack([left.T, right.T]))

    dl = w_query.shape[0]
    own_rows = key_projection_weight.shape[1]
    early = 2 * own_rows + 8
    gain_row = jnp.concatenate([attn_gain, ffn_gain])[None]
    gain_row = jnp.pad(gain_row, ((0, 7), (0, dl - gain_row.shape[1])))
    local = [pair(key_projection_weight, w_value).reshape(-1, dl), gain_row, in_rows(w_query.T)]
    kvq_z = lax.all_gather(in_rows(jnp.concatenate(local)), "z")
    kv_own = lax.all_gather(in_rows(kvq_z[:, :early]), "dp")
    q_z = in_rows(kvq_z[:, early:])
    q_own = [q_z] + [dp_xor(after(q_z, kv_own), m) for m in range(1, nd)]
    both = in_core_order(kv_own, core_swap(kv_own), 2)
    kv_weights = both[:, :, :, : 2 * own_rows].reshape(nd, nc, 2, own_rows, dl).swapaxes(1, 2)
    kv_weights = [in_rows(take(kv_weights, 0, d ^ m).reshape(-1, dl)) for m in range(nd)]
    gains = both[0, :, :, 2 * own_rows, : 2 * (width // nc)].reshape(nc, 2, -1).swapaxes(0, 1)
    gains = gains.reshape(2, 1, width).astype(F32)
    gain_attn, gain_ffn = gains[0], gains[1]

    units = w_gate.shape[1]
    down_cut = w_down.reshape(-1, 2, units, w_down.shape[1])
    down_mine, down_away = take(down_cut, 1, c), take(down_cut, 1, 1 - c)
    down_local = in_core_order(down_mine, core_swap(down_away), 2).swapaxes(0, 1).reshape(1, units, dl)
    late_local = jnp.concatenate([pair(w_gate, w_up), down_local]).reshape(-1, dl)
    late_local = in_rows(jnp.concatenate([late_local, in_rows(w_out.T)]))
    late = lax.all_gather(late_local, ("dp", "z", "core")).reshape(nd, nz, 2, -1, dl)

    lane = np.arange(128)
    frequency = jnp.power(theta_base, -jnp.asarray(lane % HALF, F32) * 2.0 / HEAD_SIZE)
    angle = positions.reshape(rows, 1).astype(F32) * frequency[None, :]
    cosine = jnp.cos(angle)
    sine = jnp.sin(angle) * jnp.asarray(np.where(lane % HEAD_SIZE < HALF, -1.0, 1.0), F32)[None, :]

    hidden_rows = hidden_in.reshape(rows, width)
    top_grad = out_grad.reshape(rows, width)
    one_blocks, kv_here = keys_values(hidden_rows, gain_attn, dp_index, kv_weights, cosine, sine)

    first_query = rank * span
    kv_up = []
    for i in range(seqs):
        piece = kv_here[i * span : (i + 1) * span]
        if i:
            piece = after(piece, kv_up[-1][1])
        kv_up.append([piece] + [z_up(piece, s) for s in range(1, nz)])

    q_own = jnp.stack([after(piece, kv_here) for piece in q_own])
    q_weights = in_core_order(q_own, core_swap(q_own), 2).reshape(nd, -1, dl)
    padding = -(QUERY_HEADS * HEAD_SIZE) % 128
    q_weights = [in_rows(jnp.pad(q_weights[m], ((0, padding), (0, 0)))) for m in range(nd)]
    one_blocks = after(one_blocks, kv_up[0][1])
    query = queries(one_blocks, dp_index, q_weights, cosine, sine)
    att_list, lse_list, kv_list, info_list, start_list = [], [], [], [], []
    for i in range(seqs):
        begin = (first_query + jnp.arange(span, dtype=jnp.int32) - positions[i]).reshape(1, span)
        info = jnp.concatenate(
            [
                jnp.stack(
                    [first_query, begin[0, 0] // block_size, (first_query + span - 1) // block_size + 1, c]
                ),
                z_index,
            ]
        ).astype(jnp.int32)
        own = [after(piece, att_list[-1]) for piece in kv_up[i]] if i else kv_up[i]
        own = jnp.stack(own)
        kv, att, lse = attend(info, begin, query[i * span : (i + 1) * span], own, core_swap(own), block_size)
        att_list.append(att)
        lse_list.append(lse)
        kv_list.append(kv)
        info_list.append(info)
        start_list.append(begin)
    late = after(late, att_list[0])
    o_weights = late[:, :, :, 3 * units :].reshape(nd, width, dl)
    o_weights = [in_rows(take(o_weights, 0, d ^ m)) for m in range(nd)]
    att_blocks, mid, two_blocks = middle(att_list, hidden_rows, gain_ffn, dp_index, o_weights)

    made, dn, ffn_grad, ffn_away = feed_forward(
        c.reshape(1).astype(jnp.int32), two_blocks, top_grad, late, units
    )
    layer_out, grad_mid, grad_att, do, ffn_sum = middle_back(
        mid, top_grad, gain_ffn, dp_index, att_blocks, made, dn, o_weights
    )

    def add(*values):
        total = values[0].astype(F32)
        for value in values[1:]:
            total = total + value.astype(F32)
        return total

    def over_dp(value):
        return add(value[0], *[dp_xor(value[m], m) for m in range(1, nd)])

    def z_pieces(value):
        return [take(value, 0, z)] + [z_shift(take(value, 0, (z + s) % nz), s) for s in range(1, nz)]

    def over_z(value):
        return add(*z_pieces(value))

    def rows_of(value, parts):
        cut = value.reshape(nd, parts, nz, 2, -1, value.shape[-1])

        def half(which):
            return take(cut, 3, which).transpose(0, 2, 1, 3, 4).reshape(nd, nz, -1, value.shape[-1])

        return half(c), half(1 - c)

    def finish(value):
        return in_rows(over_z(value.reshape(nz, -1, value.shape[-1]))).T

    ffn_grad = add(ffn_grad, after(core_swap(ffn_away), grad_att)).astype(BF)
    grad_att = after(grad_att, ffn_grad)
    ffn_grad = in_rows(ffn_grad.reshape(nd, -1, ffn_grad.shape[-1]))
    ffn_scattered = in_rows(lax.psum_scatter(ffn_grad, "dp", scatter_dimension=0, tiled=True))
    dq_list, dkv_list = [], []
    for i in range(seqs):
        here = slice(i * span, (i + 1) * span)
        grad_here = grad_att[here]
        if i:
            grad_here = after(grad_here, mine)
        dq, dkv = attend_back(
            info_list[i], start_list[i], query[here], kv_list[i], att_list[i], grad_here, lse_list[i],
            cosine[here], sine[here], block_size,
        )
        if i:
            dkv = after(dkv, *dkv_list[-1])
        cut = dkv.reshape(nz, 2, span, dkv.shape[-1])
        mine = add(take(cut, 1, c), core_swap(take(cut, 1, 1 - c))).astype(BF)
        dkv_list.append(
            [take(mine, 0, z)] + [z_down(take(mine, 0, (z - s) % nz), s) for s in range(1, nz)]
        )
        dq_list.append(dq)
    dx_blocks, dq_w = queries_back([after(dq, mine) for dq in dq_list], one_blocks, dp_index, q_weights)
    do_mine, do_other = rows_of(do, 1)
    q_mine, q_other = rows_of(dq_w[:, : QUERY_HEADS * HEAD_SIZE], 1)
    dx_blocks = after(dx_blocks, ffn_scattered, *dkv_list[-1])
    ffn_pieces = z_pieces(ffn_scattered.reshape(nz, 3, units, -1))

    input_grad, dkv_w, attn_sum = keys_values_back(
        dkv_list, one_blocks, dx_blocks, grad_mid, hidden_rows, gain_attn, dp_index, kv_weights, cosine, sine
    )
    kv_mine, kv_other = rows_of(dkv_w, 2)
    sums = jnp.concatenate([attn_sum, ffn_sum]).reshape(2, nz, 2, -1).transpose(2, 1, 0, 3).reshape(2, nz, 1, -1)
    sums = jnp.pad(sums, ((0, 0), (0, 0), (0, 7), (0, dl - sums.shape[3]))).astype(BF)

    def with_sums(value, which):
        more = jnp.broadcast_to(take(sums, 0, which)[None], (nd,) + sums.shape[1:])
        return jnp.concatenate([value, more], axis=2)

    dw_mine = jnp.concatenate([q_mine, do_mine, with_sums(kv_mine, c)], axis=2)
    dw_other = jnp.concatenate([q_other, do_other, with_sums(kv_other, 1 - c)], axis=2)
    dw = add(dw_mine, after(core_swap(dw_other), ffn_pieces[1])).astype(BF)
    dw = after(over_dp(dw).astype(BF), *ffn_pieces[2:])
    dw = in_rows(over_z(dw.reshape(nz, -1, dl)))
    q_rows = w_query.shape[1]
    w_query_grad, w_out_grad = dw[:q_rows].T, dw[q_rows : 2 * q_rows].T
    dkv_w = dw[2 * q_rows :]
    w_key_grad, w_value_grad = dkv_w[:own_rows].T, dkv_w[own_rows : 2 * own_rows].T
    gain_own = dkv_w[2 * own_rows, : 2 * (width // nc)].reshape(2, -1)
    ffn_grad = in_rows(add(*ffn_pieces)[:, :, :dl])
    w_gate_grad, w_up_grad = ffn_grad[0].T, ffn_grad[1].T
    down_cut = ffn_grad[2].reshape(units, -1, 2, w_down.shape[1]).swapaxes(0, 1)
    down_from = core_swap(take(down_cut, 2, 1 - c))
    w_down_grad = in_core_order(take(down_cut, 2, c), down_from, 1).reshape(w_down.shape)

    return (
        layer_out.reshape(seqs, span, width),
        input_grad.reshape(seqs, span, width),
        gain_own[0],
        w_query_grad,
        w_key_grad,
        w_value_grad,
        w_out_grad,
        gain_own[1],
        w_gate_grad,
        w_up_grad,
        w_down_grad,
    )


def solution(mesh):
    mesh = jax.sharding.Mesh(
        mesh.devices.reshape(mesh.shape["dp"], mesh.shape["ctx"] // 2, 2), ("dp", "z", "core")
    )
    placed = (
        P("dp", ("z", "core"), None),
        P("dp", ("z", "core")),
        P(("z", "core")),
        P("dp", ("z", "core")),
        P("dp", ("z", "core")),
        P("dp", ("z", "core")),
        P("dp", ("z", "core")),
        P(("z", "core")),
        P("dp", ("z", "core")),
        P("dp", ("z", "core")),
        P("dp", ("z", "core")),
        P("dp", ("z", "core"), None),
    )
    return jax.shard_map(
        on_device,
        mesh=mesh,
        in_specs=placed,
        out_specs=(
            P("dp", ("z", "core"), None),
            P("dp", ("z", "core"), None),
            P(("z", "core")),
            P("dp", ("z", "core")),
            P("dp", ("z", "core")),
            P("dp", ("z", "core")),
            P("dp", ("z", "core")),
            P(("z", "core")),
            P("dp", ("z", "core")),
            P("dp", ("z", "core")),
            P("dp", ("z", "core")),
        ),
        check_vma=False,
    )
```
